256 devices in a mesh: island: 64 (over z, y, core), shard: 4 (over x).
Axes of the slice: x: 4, y: 4, z: 8, core: 2. Of those that a mesh axis runs over, the one named last changes fastest.
Arguments:
- weight: bfloat16 [256, 8192], P('shard'), may hold values from -0.0625 to 0.0625
- acts_t: bfloat16 [256, 16384], P('shard', 'island')
- out_grad: bfloat16 [16384, 8192], P('island')
- momentum: bfloat16 [64, 256, 8192], P('island', 'shard'), may hold values from -6 to 6
- chosen: int32 [64, 64], P('island', 'shard'), may hold values from 0 to 16383, as said below
- counts: int32 [64, 4], P('island', 'shard'), may hold values from 1 to 16, as said below
- steps: int32 [64], P('island'), may hold values from 1 to 32
Outputs:
- update: bfloat16 [256, 8192], P('shard')
- momentum_next: bfloat16 [64, 256, 8192], P('island', 'shard')
- acts_grad: bfloat16 [256, 16384], P('shard', 'island')
The draws below stay inside these ranges and needn't reach their ends.
Inputs may be any that keep to these rules, and one draw needn't show every extreme that they name: `chosen`: row i holds, for each shard s at places s * 16 to (s + 1) * 16 - 1, distinct block numbers from s * 4096 to (s + 1) * 4096 - 1; only the first counts[i, s] of them are selected. `counts`: some device's count is 16.
All inputs are finite; a program needn't handle non-finite values.
Results may differ from the reference program's by a relative error of at most 0.001.
Values sent between devices are 32-bit elements; how exact they have to be, the bound alone decides.
No kernel may reach another device: no remote copies, remote signals or barrier semaphores. Data moves between devices by JAX's collectives and lax.ppermute only.
A program may use at most 128 MiB of HBM per device.

```python
import math
import jax
import jax.numpy as jnp
from jax import lax

D = 8192
TOKI = 256
ROWS = 256
NBLK_DEV = 4096
KMAX = 16
TOKENS = 16384
N_ISLAND = 64
N_SHARD = 4


def draw_acts_t(key, part):
    key = jax.random.fold_in(key, 11)
    rough_key = jax.random.fold_in(key, 0)
    entry_key = jax.random.fold_in(key, 1)
    ramp_key = jax.random.fold_in(key, 3)
    low_key = jax.random.fold_in(key, 4)
    high_key = jax.random.fold_in(key, 5)
    height = jnp.arange(ROWS, dtype=jnp.float32)[:, None] / ROWS
    roughness = jax.random.uniform(rough_key, (ROWS, 1), jnp.float32, 1.0, 2.5)
    island_ids = jnp.arange(N_ISLAND, dtype=jnp.int32)
    ramp_place = jax.random.uniform(ramp_key, (N_ISLAND,), jnp.float32, 0.0, 1.0)
    lowest = jax.random.randint(low_key, (), 0, N_ISLAND)
    highest = (lowest + jax.random.randint(high_key, (), 1, N_ISLAND)) % N_ISLAND
    ramp_place = jnp.where(island_ids == lowest, 0.0, jnp.where(island_ids == highest, 1.0, ramp_place))
    ramp = 0.2 * 25.0 ** ramp_place
    token_island = jnp.arange(TOKENS, dtype=jnp.int32) // TOKI
    column_ramp = ramp[token_island][None, :]
    entries = jax.random.normal(entry_key, (ROWS, TOKENS), jnp.float32)
    scaled = entries * roughness * 4.0 ** height * column_ramp / (20.0 * math.sqrt(TOKI))
    return scaled.astype(jnp.bfloat16)


def draw_out_grad(key, part):
    key = jax.random.fold_in(key, 13)
    column_key, entry_key = jax.random.split(key, 2)
    spread = jax.random.uniform(column_key, (1, D), jnp.float32, 0.0, 1.0)
    entries = jax.random.normal(entry_key, (TOKENS, D), jnp.float32)
    return (entries * 10.0 ** spread).astype(jnp.bfloat16)


def draw_chosen(key, part):
    key = jax.random.fold_in(key, 23)
    score_key, island_key = jax.random.split(key, 2)
    lists = N_ISLAND * N_SHARD
    block_ids = jnp.arange(NBLK_DEV, dtype=jnp.int32)[None, :]
    scores = jax.random.randint(score_key, (lists, NBLK_DEV), 0, 4096) * NBLK_DEV + block_ids
    marked = jax.random.randint(island_key, (), 0, N_ISLAND)
    list_ids = jnp.arange(lists, dtype=jnp.int32)[:, None]
    first_boost = (list_ids == marked * N_SHARD) & (block_ids == 0)
    last_boost = (list_ids == marked * N_SHARD + N_SHARD - 1) & (block_ids == NBLK_DEV - 1)
    scores = jnp.where(first_boost | last_boost, scores + 4096 * NBLK_DEV, scores)
    picked_scores, picked = lax.top_k(scores, KMAX)
    offsets = list_ids % N_SHARD * NBLK_DEV
    return (picked + offsets).reshape(N_ISLAND, N_SHARD * KMAX).astype(jnp.int32)


def draw_counts(key, part):
    key = jax.random.fold_in(key, 37)
    base_key, high_key, low_key = jax.random.split(key, 3)
    devices = N_ISLAND * N_SHARD
    values = jax.random.randint(base_key, (devices,), 1, KMAX + 1)
    highest = jax.random.randint(high_key, (), 0, devices)
    lowest = (highest + jax.random.randint(low_key, (), 1, devices)) % devices
    device_ids = jnp.arange(devices, dtype=jnp.int32)
    values = jnp.where(device_ids == highest, KMAX, jnp.where(device_ids == lowest, 1, values))
    return values.reshape(N_ISLAND, N_SHARD).astype(jnp.int32)


def draw_steps(key, part):
    key = jax.random.fold_in(key, 41)
    base_key, high_key, low_key = jax.random.split(key, 3)
    values = jax.random.randint(base_key, (N_ISLAND,), 1, 33)
    highest = jax.random.randint(high_key, (), 0, N_ISLAND)
    lowest = (highest + jax.random.randint(low_key, (), 1, N_ISLAND)) % N_ISLAND
    island_ids = jnp.arange(N_ISLAND, dtype=jnp.int32)
    values = jnp.where(island_ids == highest, 32, jnp.where(island_ids == lowest, 1, values))
    return values.astype(jnp.int32)


def steps_of(rng, extent, shards, smallest, top_value):
    factor_of = 1.0
    for dim, shards_of in shards:
        draws = jax.random.uniform(jax.random.fold_in(jax.random.fold_in(rng, 6), dim), (shards_of,), jnp.float32, smallest / len(shards), top_value / len(shards))
        factor_of = factor_of * jnp.repeat(jnp.exp(draws), extent[dim] // shards_of).reshape((-1,) + (1,) * (len(extent) - 1 - dim))
    return factor_of


def normal_values(own_key, dims, width, bound, pieces=(), kind=jnp.bfloat16):
    drawn = jax.random.normal(own_key, dims, jnp.float32) * width
    if len(pieces) > 0:
        drawn = steps_of(own_key, dims, pieces, -0.22, 0.18) * drawn
    return jnp.clip(drawn, min=-bound, max=bound).astype(kind)


def setup_inputs(seed: int = 0) -> dict:
    keys = jax.random.split(jax.random.key(seed), 8)
    weight = normal_values(keys[0], (ROWS, D), D ** -0.5, 0.0625, ((0, 4),))
    acts_t = draw_acts_t(jax.random.fold_in(keys[7], 71), 0)
    out_grad = draw_out_grad(jax.random.fold_in(keys[7], 71), 0)
    momentum = normal_values(keys[3], (N_ISLAND, ROWS, D), 1.0, 6.0, ((0, 64), (1, 4)))
    chosen = draw_chosen(jax.random.fold_in(keys[7], 71), 0)
    counts = draw_counts(jax.random.fold_in(keys[7], 71), 0)
    steps = draw_steps(jax.random.fold_in(keys[7], 71), 0)
    return dict(weight=weight, acts_t=acts_t, out_grad=out_grad, momentum=momentum, chosen=chosen, counts=counts, steps=steps)


def cosine_table():
    freq = jnp.arange(64, dtype=jnp.float32)[:, None]
    place = jnp.arange(64, dtype=jnp.float32)[None, :]
    waves = jnp.cos(jnp.pi * (2.0 * place + 1.0) * freq / 128.0)
    return jnp.where(freq == 0.0, 0.125, math.sqrt(2.0 / 64.0)) * waves

def forward_tiles(matrix, cosine):
    row_count, column_count = matrix.shape
    tiles = matrix.reshape(row_count // 64, 64, column_count // 64, 64)
    result = jnp.einsum('ij,ajbk,lk->aibl', cosine, tiles, cosine, precision=lax.Precision.HIGHEST)
    return result.reshape(row_count, column_count)

def inverse_tiles(matrix, cosine):
    row_count, column_count = matrix.shape
    tiles = matrix.reshape(row_count // 64, 64, column_count // 64, 64)
    result = jnp.einsum('ji,ajbk,kl->aibl', cosine, tiles, cosine, precision=lax.Precision.HIGHEST)
    return result.reshape(row_count, column_count)

def to_blocks(matrix):
    row_count, column_count = matrix.shape
    shaped = matrix.reshape(row_count // 8, 8, column_count // 16, 16)
    return shaped.transpose(0, 2, 1, 3).reshape(-1, 128)

def from_blocks(blocks, row_count, column_count):
    shaped = blocks.reshape(row_count // 8, column_count // 16, 8, 16)
    return shaped.transpose(0, 2, 1, 3).reshape(row_count, column_count)

def reference(weight, acts_t, out_grad, momentum, chosen, counts, steps):
    cosine = cosine_table()
    row_count, column_count = weight.shape
    block_count = row_count * column_count // 128
    slot_count = chosen.shape[1] // N_SHARD
    step_values = steps.astype(jnp.float32)
    shares = N_ISLAND * step_values / jnp.sum(step_values)
    acts_split = acts_t.reshape(row_count, N_ISLAND, TOKI).transpose(1, 0, 2)
    grads_split = out_grad.reshape(N_ISLAND, TOKI, column_count)
    live_slots = jnp.arange(slot_count, dtype=jnp.int32)[None, None, :] < counts[:, :, None]
    live_slots = live_slots.reshape(N_ISLAND, N_SHARD * slot_count).astype(jnp.float32)

    def island_step(running, inputs):
        island_acts, island_grads, island_momentum, island_picks, island_live, island_share = inputs
        grad_weight = jnp.dot(island_acts, island_grads, preferred_element_type=jnp.float32)
        backward = lax.dot_general(weight, island_grads, (((1,), (1,)), ((), ())), preferred_element_type=jnp.float32).astype(jnp.bfloat16)
        root_mean = jnp.sqrt(jnp.mean(grad_weight * grad_weight) + 1e-06)
        factor = jnp.minimum(1.0, 1.0 / root_mean)
        combined = 0.9 * island_momentum.astype(jnp.float32) + factor * grad_weight
        blocks = to_blocks(forward_tiles(combined, cosine))
        picked = jnp.zeros((block_count,), jnp.float32).at[island_picks].max(island_live)
        remaining = blocks * (1.0 - picked)[:, None]
        kept_momentum = inverse_tiles(from_blocks(remaining, row_count, column_count), cosine).astype(jnp.bfloat16)
        running = running + island_share * (blocks * picked[:, None])
        return (running, (kept_momentum, backward))
    start_grid = jnp.zeros((block_count, 128), jnp.float32)
    merged, (momentum_next, backward_all) = lax.scan(island_step, start_grid, (acts_split, grads_split, momentum, chosen, live_slots, shares))
    update = inverse_tiles(from_blocks(merged, row_count, column_count), cosine).astype(jnp.bfloat16)
    acts_grad = backward_all.transpose(1, 0, 2).reshape(row_count, N_ISLAND * TOKI)
    return (update, momentum_next, acts_grad)
```

```python
import functools

import jax
import jax.numpy as jnp
import ml_dtypes
import numpy as np
from jax import lax
from jax.experimental import pallas as pl
from jax.experimental.pallas import tpu as pltpu
from jax.sharding import PartitionSpec as P

BF = jnp.bfloat16
F32 = jnp.float32
SLOTS = 16
PAY = SLOTS * 128
MIB = 1 << 20


def dct_matrix():
    freq = np.arange(64, dtype=np.float64)[:, None]
    place = np.arange(64, dtype=np.float64)[None, :]
    waves = np.cos(np.pi * (2.0 * place + 1.0) * freq / 128.0)
    return np.where(freq == 0.0, 0.125, np.sqrt(2.0 / 64.0)) * waves


def halves(a):
    hi = a.astype(ml_dtypes.bfloat16)
    lo = (a - hi.astype(np.float64)).astype(ml_dtypes.bfloat16)
    return hi, lo


COS = dct_matrix()
COS_HI, COS_LO = halves(COS)
INV_HI, INV_LO = halves(COS.T)


def diagonal(a, copies):
    return np.kron(np.eye(copies), a.astype(np.float64)).astype(ml_dtypes.bfloat16)


FWD_LEFT3 = np.concatenate([COS_HI, COS_HI, COS_LO], 1)
FWD_LEFT2 = np.concatenate([COS_HI, COS_LO], 1)
INV_LEFT3 = np.concatenate([INV_HI, INV_HI, INV_LO], 1)
FWD_RIGHT3 = np.concatenate([diagonal(COS_HI.T, 2), diagonal(COS_HI.T, 2), diagonal(COS_LO.T, 2)], 0)
INV_RIGHT3 = np.concatenate([diagonal(COS_HI, 2), diagonal(COS_HI, 2), diagonal(COS_LO, 2)], 0)
INV_WIDE_HI = diagonal(COS_HI, 4)
INV_WIDE_LO = diagonal(COS_LO, 4)


def split(x):
    hi = x.astype(BF)
    return hi, (x - hi.astype(F32)).astype(BF)


def dot(a, b):
    return jnp.dot(a, b, preferred_element_type=F32)


def grad_kernel(acts, og, grad, squares, total):
    step = pl.program_id(0)

    @pl.when(step == 0)
    def _():
        total[...] = jnp.zeros_like(total)

    g = dot(acts[...], og[...])
    grad[...] = g
    rows, width = g.shape
    total[...] += jnp.sum((g * g).reshape(rows // 8, 8, width), axis=0)

    @pl.when(step == pl.num_programs(0) - 1)
    def _():
        squares[...] = jnp.full(squares.shape, jnp.sum(total[...]), F32)


def grad_call(acts, og, chunk=1024):
    rows, toks = acts.shape
    cols = og.shape[1]
    return pl.pallas_call(
        grad_kernel,
        grid=(cols // chunk,),
        in_specs=[
            pl.BlockSpec((rows, toks), lambda i: (0, 0)),
            pl.BlockSpec((toks, chunk), lambda i: (0, i)),
        ],
        out_specs=[
            pl.BlockSpec((rows, chunk), lambda i: (0, i)),
            pl.BlockSpec((1, 128), lambda i: (0, 0)),
        ],
        out_shape=[
            jax.ShapeDtypeStruct((rows, cols), F32),
            jax.ShapeDtypeStruct((1, 128), F32),
        ],
        scratch_shapes=[pltpu.VMEM((8, chunk), F32)],
        compiler_params=pltpu.CompilerParams(vmem_limit_bytes=24 * MIB),
        cost_estimate=pl.CostEstimate(flops=2 * rows * toks * cols, bytes_accessed=6 * MIB, transcendentals=0),
        name="weight_grad",
    )(acts, og)


def acts_grad_kernel(weight, og, out, total):
    step = pl.program_id(0)

    @pl.when(step == 0)
    def _():
        total[...] = jnp.zeros_like(total)

    total[...] += lax.dot_general(
        weight[...], og[...], (((1,), (1,)), ((), ())), preferred_element_type=F32
    )

    @pl.when(step == pl.num_programs(0) - 1)
    def _():
        out[...] = total[...].astype(BF)


def acts_grad_call(weight, og, chunk=1024):
    rows, cols = weight.shape
    toks = og.shape[0]
    return pl.pallas_call(
        acts_grad_kernel,
        grid=(cols // chunk,),
        in_specs=[
            pl.BlockSpec((rows, chunk), lambda i: (0, i)),
            pl.BlockSpec((toks, chunk), lambda i: (0, i)),
        ],
        out_specs=pl.BlockSpec((rows, toks), lambda i: (0, 0)),
        out_shape=jax.ShapeDtypeStruct((rows, toks), BF),
        scratch_shapes=[pltpu.VMEM((rows, toks), F32)],
        compiler_params=pltpu.CompilerParams(vmem_limit_bytes=24 * MIB),
        cost_estimate=pl.CostEstimate(flops=2 * rows * toks * cols, bytes_accessed=5 * MIB, transcendentals=0),
        name="acts_grad",
    )(weight, og)


def lane_group(shape):
    return lax.broadcasted_iota(jnp.int32, shape, 1) >> 4


def coef_kernel(picks, counts, momentum, grad, left2, left3, right3,
                coef_m, coef_g, pack_m, pack_g,
                mom_in, grad_in, side_m, side_g, low, sem):
    def copies(j):
        pair = (picks[j] >> 3) & 63
        cols = pl.ds(pl.multiple_of(pair * 128, 128), 128)
        here = pl.ds(j * 128, 128)
        return (
            pltpu.make_async_copy(momentum.at[:, cols], mom_in.at[:, here], sem.at[0, j]),
            pltpu.make_async_copy(grad.at[:, cols], grad_in.at[:, here], sem.at[1, j]),
        )

    for j in range(SLOTS):
        for c in copies(j):
            c.start()
    for j in range(SLOTS):
        for c in copies(j):
            c.wait()
    m = mom_in[...]
    g_hi, g_lo = split(grad_in[...])
    side_m[...] = dot(left2[...], jnp.concatenate([m, m], 0))
    side_g[...] = dot(left3[...], jnp.concatenate([g_hi, g_lo, g_hi], 0))
    for j in range(SLOTS):
        rows = pl.ds(pl.multiple_of((picks[j] >> 9) * 8, 8), 8)
        low[8 * j:8 * j + 8, :] = side_m[rows, 128 * j:128 * j + 128]
        low[128 + 8 * j:136 + 8 * j, :] = side_g[rows, 128 * j:128 * j + 128]
    hi, lo = split(low[...])
    low[...] = dot(jnp.concatenate([hi, lo, hi], 1), right3[...])
    group = lane_group((8, 128))
    live = counts[0]
    for base, coef, pack in ((0, coef_m, pack_m), (128, coef_g, pack_g)):
        packed = [jnp.zeros((8, 128), F32)] * 2
        for j in range(SLOTS):
            off = picks[j] & 7
            want = jnp.where(j < live, off, 8)
            kept = jnp.where(group == want, low[base + 8 * j:base + 8 * j + 8, :], 0.0)
            coef[8 * j:8 * j + 8, :] = kept
            turned = pltpu.roll(kept, ((j % 8 - off) & 7) * 16, 1)
            packed[j // 8] = packed[j // 8] + turned
        pack[0:8, :] = packed[0]
        pack[8:16, :] = packed[1]


def coef_call(picks, counts, momentum, grad):
    rows, cols = grad.shape
    vm = pl.BlockSpec(memory_space=pltpu.VMEM)
    sm = pl.BlockSpec(memory_space=pltpu.SMEM)
    anyw = pl.BlockSpec(memory_space=pl.ANY)
    return pl.pallas_call(
        coef_kernel,
        in_specs=[sm, sm, anyw, anyw, vm, vm, vm],
        out_specs=[vm] * 4,
        out_shape=[
            jax.ShapeDtypeStruct((128, 128), F32),
            jax.ShapeDtypeStruct((128, 128), F32),
            jax.ShapeDtypeStruct((16, 128), F32),
            jax.ShapeDtypeStruct((16, 128), F32),
        ],
        scratch_shapes=[
            pltpu.VMEM((rows, PAY), BF),
            pltpu.VMEM((rows, PAY), F32),
            pltpu.VMEM((rows, PAY), F32),
            pltpu.VMEM((rows, PAY), F32),
            pltpu.VMEM((256, 128), F32),
            pltpu.SemaphoreType.DMA((2, SLOTS)),
        ],
        compiler_params=pltpu.CompilerParams(vmem_limit_bytes=24 * MIB),
        cost_estimate=pl.CostEstimate(flops=200_000_000, bytes_accessed=3 * MIB, transcendentals=0),
        name="selected_coefs",
    )(picks, counts, momentum, grad, FWD_LEFT2, FWD_LEFT3, FWD_RIGHT3)


def rest_kernel(picks, factor, coef_m, coef_g, momentum, grad, left3, right3, out, full, wide):
    f = factor[0]
    wide[...] = jnp.zeros_like(wide)
    hi, lo = split(0.9 * coef_m[...] + f * coef_g[...])
    low = dot(jnp.concatenate([hi, lo, hi], 1), right3[...])
    for j in range(SLOTS):
        rows = pl.ds(pl.multiple_of((picks[j] >> 9) * 8, 8), 8)
        wide[rows, 128 * j:128 * j + 128] = low[8 * j:8 * j + 8, :]
    hi, lo = split(wide[...])
    wide[...] = dot(left3[...], jnp.concatenate([hi, lo, hi], 0))
    cols = full.shape[1]
    for c in range(0, cols, 1024):
        at = slice(c, c + 1024)
        full[:, at] = 0.9 * momentum[:, at].astype(F32) + f * grad[:, at]
    for j in range(SLOTS):
        pair = (picks[j] >> 3) & 63
        at = pl.ds(pl.multiple_of(pair * 128, 128), 128)
        full[:, at] = full[:, at] - wide[:, 128 * j:128 * j + 128]
    for c in range(0, cols, 1024):
        at = slice(c, c + 1024)
        out[:, at] = full[:, at].astype(BF)


def rest_call(picks, factor, coef_m, coef_g, momentum, grad):
    rows, cols = grad.shape
    vm = pl.BlockSpec(memory_space=pltpu.VMEM)
    sm = pl.BlockSpec(memory_space=pltpu.SMEM)
    return pl.pallas_call(
        rest_kernel,
        in_specs=[sm, sm] + [vm] * 6,
        out_specs=vm,
        out_shape=jax.ShapeDtypeStruct((rows, cols), BF),
        scratch_shapes=[pltpu.VMEM((rows, cols), F32), pltpu.VMEM((rows, PAY), F32)],
        compiler_params=pltpu.CompilerParams(vmem_limit_bytes=24 * MIB),
        cost_estimate=pl.CostEstimate(flops=100_000_000, bytes_accessed=4 * MIB, transcendentals=0),
        name="momentum_rest",
    )(picks, factor, coef_m, coef_g, momentum, grad, INV_LEFT3, INV_RIGHT3)


def merge_kernel(picks, scale, own, other, left3, wide_hi, wide_lo, out, grid, side):
    grid[...] = jnp.zeros_like(grid)
    group = lane_group((8, 128))
    islands = own.shape[0]

    def add_islands(pay, first):
        def one(i, carry):
            tiles = [pay[i, 0:8, :], pay[i, 8:16, :]]
            base = (first + i) * SLOTS
            olds, news, masks, places = [], [], [], []
            for j in range(SLOTS):
                b = picks[base + j]
                off = b & 7
                place = b >> 3
                turned = pltpu.roll(tiles[j // 8], ((off - j % 8) & 7) * 16, 1)
                olds.append(grid[place])
                news.append(turned)
                masks.append(group == off)
                places.append(place)
            for j in range(SLOTS):
                pltpu.store(grid.at[places[j]], olds[j] + news[j], mask=masks[j])
            return carry

        lax.fori_loop(0, islands, one, 0)

    add_islands(own, 0)
    add_islands(other, islands)
    s = scale[0]
    pairs = grid.shape[0] // 8

    def left(c, carry):
        parts = []
        for k in range(2):
            parts.append(jnp.concatenate([grid[r * pairs + 2 * c + k] for r in range(8)], 0))
        hi, lo = split(jnp.concatenate(parts, 1))
        z = dot(left3[...], jnp.concatenate([hi, lo, hi], 0)) * s
        hi, lo = split(z)
        y = dot(hi, wide_hi[...]) + (dot(lo, wide_hi[...]) + dot(hi, wide_lo[...]))
        out[:, pl.ds(pl.multiple_of(c * 256, 256), 256)] = y.astype(BF)
        return carry

    lax.fori_loop(0, pairs // 2, left, 0, unroll=4)


def merge_call(picks, scale, own, other, rows, cols):
    vm = pl.BlockSpec(memory_space=pltpu.VMEM)
    sm = pl.BlockSpec(memory_space=pltpu.SMEM)
    return pl.pallas_call(
        merge_kernel,
        in_specs=[sm, sm] + [vm] * 5,
        out_specs=vm,
        out_shape=jax.ShapeDtypeStruct((rows, cols), BF),
        scratch_shapes=[pltpu.VMEM((rows * cols // 1024, 8, 128), F32), pltpu.VMEM((8, 128), F32)],
        compiler_params=pltpu.CompilerParams(vmem_limit_bytes=24 * MIB),
        cost_estimate=pl.CostEstimate(flops=1_000_000_000, bytes_accessed=2 * MIB, transcendentals=0),
        name="merge_update",
    )(picks, scale, own, other, INV_LEFT3, INV_WIDE_HI, INV_WIDE_LO)


def on_device(weight, acts_t, out_grad, momentum, chosen, counts, steps):
    rows, cols = weight.shape
    islands = lax.axis_size("island")
    shards = lax.axis_size("shard")
    half = islands // 2
    same_core = [[2 * i + c for i in range(half)] for c in range(2)]
    other_core = [(i, i ^ 1) for i in range(islands)]
    momentum = momentum[0]

    picks = chosen[0] - lax.axis_index("shard") * (rows * cols // 128)
    live = counts[0]

    grad, squares = grad_call(acts_t, out_grad)
    squares = squares + lax.ppermute(squares, "shard", [(i, i ^ 1) for i in range(shards)])
    acts_grad = acts_grad_call(weight, out_grad)
    squares = squares + lax.ppermute(squares, "shard", [(i, i ^ 2) for i in range(shards)])
    coef_m, coef_g, pack_m, pack_g = coef_call(picks, live, momentum, grad)

    mean = squares[0, :1] / float(rows * cols * shards)
    factor = jnp.minimum(1.0, 1.0 / jnp.sqrt(mean + 1e-06))
    own_steps = steps.astype(F32)
    payload = (0.9 * pack_m + factor * pack_g) * own_steps
    meta = jnp.concatenate([picks.astype(F32), own_steps, jnp.zeros((111,), F32)])
    sent = jnp.concatenate([payload.reshape(1, PAY), meta[None]], 1)
    sent = jnp.broadcast_to(sent[None], (half, 1, PAY + 128))
    got = lax.all_to_all(sent, "island", 0, 0, tiled=True, axis_index_groups=same_core)
    swapped = lax.ppermute(got, "island", other_core)

    momentum_next = rest_call(picks, factor, coef_m, coef_g, momentum, grad)

    metas = jnp.concatenate([got[:, 0, PAY:PAY + 17], swapped[:, 0, PAY:PAY + 17]], 0)
    scale = (islands / jnp.sum(metas[:, 16]))[None]
    all_picks = metas[:, :16].astype(jnp.int32).reshape(-1)
    update = merge_call(
        all_picks, scale,
        got[:, 0, :PAY].reshape(half, SLOTS, 128),
        swapped[:, 0, :PAY].reshape(half, SLOTS, 128),
        rows, cols,
    )
    return (update, momentum_next[None], acts_grad)


def solution(mesh):
    placed = (
        P("shard", None),
        P("shard", "island"),
        P("island", None),
        P("island", "shard", None),
        P("island", "shard"),
        P("island", "shard"),
        P("island"),
    )
    return jax.shard_map(
        on_device,
        mesh=mesh,
        in_specs=placed,
        out_specs=(P("shard", None), P("island", "shard", None), P("shard", "island")),
        check_vma=False,
    )
```

```python
import functools

import jax
import jax.numpy as jnp
import ml_dtypes
import numpy as np
from jax import lax
from jax.experimental import pallas as pl
from jax.experimental.pallas import tpu as pltpu
from jax.sharding import PartitionSpec as P

BF = jnp.bfloat16
F32 = jnp.float32
SLOTS = 16
PAY = SLOTS * 128
MIB = 1 << 20


def dct_matrix():
    freq = np.arange(64, dtype=np.float64)[:, None]
    place = np.arange(64, dtype=np.float64)[None, :]
    waves = np.cos(np.pi * (2.0 * place + 1.0) * freq / 128.0)
    return np.where(freq == 0.0, 0.125, np.sqrt(2.0 / 64.0)) * waves


def halves(a):
    hi = a.astype(ml_dtypes.bfloat16)
    lo = (a - hi.astype(np.float64)).astype(ml_dtypes.bfloat16)
    return hi, lo


COS = dct_matrix()
COS_HI, COS_LO = halves(COS)
INV_HI, INV_LO = halves(COS.T)


def diagonal(a, copies):
    return np.kron(np.eye(copies), a.astype(np.float64)).astype(ml_dtypes.bfloat16)


FWD_LEFT3 = np.concatenate([COS_HI, COS_HI, COS_LO], 1)
FWD_LEFT2 = np.concatenate([COS_HI, COS_LO], 1)
INV_LEFT3 = np.concatenate([INV_HI, INV_HI, INV_LO], 1)
FWD_RIGHT3 = np.concatenate([diagonal(COS_HI.T, 2), diagonal(COS_HI.T, 2), diagonal(COS_LO.T, 2)], 0)
INV_RIGHT3 = np.concatenate([diagonal(COS_HI, 2), diagonal(COS_HI, 2), diagonal(COS_LO, 2)], 0)
INV_WIDE_HI = diagonal(COS_HI, 4)
INV_WIDE_LO = diagonal(COS_LO, 4)


def split(x):
    hi = x.astype(BF)
    return hi, (x - hi.astype(F32)).astype(BF)


def dot(a, b):
    return jnp.dot(a, b, preferred_element_type=F32)


PARTS = 2


def grad_kernel(acts, og, weight, grad, squares, og_in, weight_in, acts_in, sem):
    cols = og_in.shape[1]
    width = cols // PARTS
    first = pltpu.make_async_copy(acts, acts_in, sem.at[PARTS])
    first.start()
    parts = []
    for i in range(PARTS):
        at = slice(i * width, (i + 1) * width)
        parts.append(pltpu.make_async_copy(og.at[:, at], og_in.at[:, at], sem.at[i]))
        parts[i].start()
    last = pltpu.make_async_copy(weight, weight_in, sem.at[PARTS + 1])
    last.start()
    first.wait()
    a = acts_in[...]
    total = jnp.zeros((8, 512), F32)
    for i in range(PARTS):
        at = slice(i * width, (i + 1) * width)
        parts[i].wait()
        g = dot(a, og_in[:, at])
        grad[:, at] = g
        g = jnp.sum((g * g).reshape(-1, 8, width), axis=0)
        for k in range(0, width, 512):
            total = total + g[:, k:k + 512]
    squares[...] = jnp.full(squares.shape, jnp.sum(total), F32)
    last.wait()


def grad_call(acts, og, weight):
    rows, toks = acts.shape
    cols = og.shape[1]
    vm = pl.BlockSpec(memory_space=pltpu.VMEM)
    anyw = pl.BlockSpec(memory_space=pl.ANY)
    held = [pltpu.with_memory_space_constraint(x, pltpu.HBM) for x in (acts, og, weight)]
    return pl.pallas_call(
        grad_kernel,
        in_specs=[anyw] * 3,
        out_specs=[vm] * 4,
        out_shape=[
            jax.ShapeDtypeStruct((rows, cols), F32),
            jax.ShapeDtypeStruct((1, 128), F32),
            jax.ShapeDtypeStruct((toks, cols), BF),
            jax.ShapeDtypeStruct((rows, cols), BF),
        ],
        scratch_shapes=[
            pltpu.VMEM((rows, toks), BF),
            pltpu.SemaphoreType.DMA((PARTS + 2,)),
        ],
        compiler_params=pltpu.CompilerParams(vmem_limit_bytes=24 * MIB),
        cost_estimate=pl.CostEstimate(flops=2 * rows * toks * cols, bytes_accessed=6 * MIB, transcendentals=0),
        name="weight_grad",
    )(*held)


def acts_grad_kernel(weight, og, out):
    total = lax.dot_general(og[...], weight[...], (((1,), (1,)), ((), ())), preferred_element_type=F32)
    out[...] = total.T.astype(BF)


def acts_grad_call(weight, og):
    rows, cols = weight.shape
    toks = og.shape[0]
    vm = pl.BlockSpec(memory_space=pltpu.VMEM)
    return pl.pallas_call(
        acts_grad_kernel,
        in_specs=[vm, vm],
        out_specs=vm,
        out_shape=jax.ShapeDtypeStruct((rows, toks), BF),
        compiler_params=pltpu.CompilerParams(vmem_limit_bytes=16 * MIB),
        cost_estimate=pl.CostEstimate(flops=2 * rows * toks * cols, bytes_accessed=5 * MIB, transcendentals=0),
        name="acts_grad",
    )(weight, og)


def lane_group(shape):
    return lax.broadcasted_iota(jnp.int32, shape, 1) >> 4


def coef_kernel(picks, counts, momentum, grad, left2, left3, right3, back_left3, back_right3,
                pack_m, pack_g, rest_m, rest_g,
                mom_in, grad_in, side_m, side_g, low, wide):
    pairs = [(picks[j] >> 3) & 63 for j in range(SLOTS)]
    lanes = [pl.ds(pl.multiple_of(p * 128, 128), 128) for p in pairs]
    tops = [pl.ds(pl.multiple_of((picks[j] >> 9) * 8, 8), 8) for j in range(SLOTS)]
    offs = [picks[j] & 7 for j in range(SLOTS)]
    here = [slice(128 * j, 128 * j + 128) for j in range(SLOTS)]
    for j in range(SLOTS):
        mom_in[:, here[j]] = momentum[:, lanes[j]]
        grad_in[:, here[j]] = grad[:, lanes[j]]
    wide[...] = jnp.zeros_like(wide)
    m = mom_in[...]
    g_hi, g_lo = split(grad_in[...])
    side_m[...] = dot(left2[...], jnp.concatenate([m, m], 0))
    side_g[...] = dot(left3[...], jnp.concatenate([g_hi, g_lo, g_hi], 0))
    for j in range(SLOTS):
        low[8 * j:8 * j + 8, :] = side_m[tops[j], here[j]]
        low[128 + 8 * j:136 + 8 * j, :] = side_g[tops[j], here[j]]
    hi, lo = split(low[...])
    low[...] = dot(jnp.concatenate([hi, lo, hi], 1), right3[...])
    group = lane_group((8, 128))
    live = counts[0]
    wants = [jnp.where(j < live, offs[j], 8) for j in range(SLOTS)]
    for base, pack in ((0, pack_m), (128, pack_g)):
        packed = [jnp.zeros((8, 128), F32)] * 2
        for j in range(SLOTS):
            at = slice(base + 8 * j, base + 8 * j + 8)
            kept = jnp.where(group == wants[j], low[at, :], 0.0)
            low[at, :] = kept
            packed[j // 8] = packed[j // 8] + pltpu.roll(kept, ((j % 8 - offs[j]) & 7) * 16, 1)
        pack[0:8, :] = packed[0]
        pack[8:16, :] = packed[1]
    hi, lo = split(low[...])
    low[...] = dot(jnp.concatenate([hi, lo, hi], 1), back_right3[...])
    for j in range(SLOTS):
        wide[tops[j], 128 * j:128 * j + 128] = low[8 * j:8 * j + 8, :]
        wide[tops[j], PAY + 128 * j:PAY + 128 * j + 128] = low[128 + 8 * j:136 + 8 * j, :]
    hi, lo = split(wide[...])
    wide[...] = dot(back_left3[...], jnp.concatenate([hi, lo, hi], 0))
    cols = grad.shape[1]
    for c in range(0, cols, 1024):
        at = slice(c, c + 1024)
        rest_m[:, at] = 0.9 * momentum[:, at].astype(F32)
        rest_g[:, at] = grad[:, at]
    for j in range(SLOTS):
        rest_m[:, lanes[j]] = rest_m[:, lanes[j]] - 0.9 * wide[:, 128 * j:128 * j + 128]
        rest_g[:, lanes[j]] = rest_g[:, lanes[j]] - wide[:, PAY + 128 * j:PAY + 128 * j + 128]


def coef_call(picks, counts, momentum, grad):
    rows, cols = grad.shape
    vm = pl.BlockSpec(memory_space=pltpu.VMEM)
    sm = pl.BlockSpec(memory_space=pltpu.SMEM)
    return pl.pallas_call(
        coef_kernel,
        in_specs=[sm, sm] + [vm] * 7,
        out_specs=[vm] * 4,
        out_shape=[
            jax.ShapeDtypeStruct((16, 128), F32),
            jax.ShapeDtypeStruct((16, 128), F32),
            jax.ShapeDtypeStruct((rows, cols), F32),
            jax.ShapeDtypeStruct((rows, cols), F32),
        ],
        scratch_shapes=[
            pltpu.VMEM((rows, PAY), BF),
            pltpu.VMEM((rows, PAY), F32),
            pltpu.VMEM((rows, PAY), F32),
            pltpu.VMEM((rows, PAY), F32),
            pltpu.VMEM((256, 128), F32),
            pltpu.VMEM((rows, 2 * PAY), F32),
        ],
        compiler_params=pltpu.CompilerParams(vmem_limit_bytes=24 * MIB),
        cost_estimate=pl.CostEstimate(flops=300_000_000, bytes_accessed=8 * MIB, transcendentals=0),
        name="selected_coefs",
    )(picks, counts, momentum, grad, FWD_LEFT2, FWD_LEFT3, FWD_RIGHT3, INV_LEFT3, INV_RIGHT3)


GROUP = 16


def add_islands(got, grid, ints, picks, sem):
    ints[...] = got[:, :, PAY:].astype(jnp.int32)
    to_scalars = pltpu.make_async_copy(ints, picks, sem)
    to_scalars.start()
    grid[...] = jnp.zeros_like(grid)
    steps = jnp.sum(got[:, :, PAY + SLOTS:PAY + SLOTS + 1])
    to_scalars.wait()
    group = lane_group((8, 128))

    def one(i, carry):
        tiles = [got[i, 0, 1024 * t:1024 * t + 1024].reshape(8, 128) for t in range(2)]
        olds, news, masks, places = [], [], [], []
        for j in range(SLOTS):
            b = picks[i, 0, j]
            off = b & 7
            place = b >> 3
            news.append(pltpu.roll(tiles[j // 8], ((off - j % 8) & 7) * 16, 1))
            olds.append(grid[place])
            masks.append(group == off)
            places.append(place)
        for j in range(SLOTS):
            pltpu.store(grid.at[places[j]], olds[j] + news[j], mask=masks[j])
        return carry

    lax.fori_loop(0, got.shape[0], one, 0, unroll=4)
    return steps


def scatter_kernel(got, grid, steps, ints, picks, sem):
    steps[...] = jnp.full(steps.shape, add_islands(got, grid, ints, picks, sem), F32)


def scatter_call(got, rows, cols):
    vm = pl.BlockSpec(memory_space=pltpu.VMEM)
    islands = got.shape[0]
    return pl.pallas_call(
        scatter_kernel,
        in_specs=[vm],
        out_specs=[vm, vm],
        out_shape=[
            jax.ShapeDtypeStruct((rows * cols // 1024, 8, 128), F32),
            jax.ShapeDtypeStruct((1, 128), F32),
        ],
        scratch_shapes=[
            pltpu.VMEM((islands, 1, 128), jnp.int32),
            pltpu.SMEM((islands, 1, 128), jnp.int32),
            pltpu.SemaphoreType.DMA,
        ],
        compiler_params=pltpu.CompilerParams(vmem_limit_bytes=16 * MIB),
        cost_estimate=pl.CostEstimate(flops=300_000_000, bytes_accessed=8 * MIB, transcendentals=0),
        name="scatter_own",
    )(got)


def merge_kernel(got, first, first_steps, left3, wide_hi, wide_lo, out, grid, ints, picks, done, sem, out_sem):
    islands = 2.0 * got.shape[0]
    steps = add_islands(got, grid, ints, picks, sem)
    s = islands / (steps + first_steps[0, 0])
    pairs = grid.shape[0] // 8
    width = 256 * GROUP
    copies = []
    for q in range(pairs // (2 * GROUP)):
        parts = []
        for k in range(2 * GROUP):
            at = [r * pairs + 2 * GROUP * q + k for r in range(8)]
            parts.append(jnp.concatenate([grid[p] + first[p] for p in at], 0))
        hi, lo = split(jnp.concatenate(parts, 1))
        z = dot(left3[...], jnp.concatenate([hi, lo, hi], 0)) * s
        z = jnp.concatenate([z[:, 256 * k:256 * k + 256] for k in range(GROUP)], 0)
        hi, lo = split(z)
        y = dot(hi, wide_hi[...]) + (dot(lo, wide_hi[...]) + dot(hi, wide_lo[...]))
        y = y.astype(BF)
        for k in range(GROUP):
            at = 256 * (GROUP * q + k)
            done[:, at:at + 256] = y[64 * k:64 * k + 64]
        at = slice(width * q, width * q + width)
        copies.append(pltpu.make_async_copy(done.at[:, at], out.at[:, at], out_sem.at[q]))
        copies[q].start()
    for c in copies:
        c.wait()


def merge_call(got, first, first_steps, rows, cols):
    vm = pl.BlockSpec(memory_space=pltpu.VMEM)
    anyw = pl.BlockSpec(memory_space=pl.ANY)
    islands = got.shape[0]
    return pl.pallas_call(
        merge_kernel,
        in_specs=[vm] * 6,
        out_specs=anyw,
        out_shape=jax.ShapeDtypeStruct((rows, cols), BF),
        scratch_shapes=[
            pltpu.VMEM((rows * cols // 1024, 8, 128), F32),
            pltpu.VMEM((islands, 1, 128), jnp.int32),
            pltpu.SMEM((islands, 1, 128), jnp.int32),
            pltpu.VMEM((rows, cols), BF),
            pltpu.SemaphoreType.DMA,
            pltpu.SemaphoreType.DMA((cols // (256 * GROUP),)),
        ],
        compiler_params=pltpu.CompilerParams(vmem_limit_bytes=32 * MIB),
        cost_estimate=pl.CostEstimate(flops=1_000_000_000, bytes_accessed=2 * MIB, transcendentals=0),
        name="merge_update",
    )(got, first, first_steps, INV_LEFT3, INV_WIDE_HI, INV_WIDE_LO)


def on_device(weight, acts_t, out_grad, momentum, chosen, counts, steps):
    rows, cols = weight.shape
    islands = lax.axis_size("island")
    shards = lax.axis_size("shard")
    half = islands // 2
    same_core = [[2 * i + c for i in range(half)] for c in range(2)]
    other_core = [(i, i ^ 1) for i in range(islands)]
    momentum = momentum[0]

    picks = chosen[0] % (rows * cols // 128)
    live = counts[0]

    grad, squares, og_held, weight_held = grad_call(acts_t, out_grad, weight)
    squares = squares + lax.ppermute(squares, "shard", [(i, i ^ 1) for i in range(shards)])
    acts_grad = acts_grad_call(weight_held, og_held)
    squares, acts_grad = lax.optimization_barrier((squares, acts_grad))
    squares = squares + lax.ppermute(squares, "shard", [(i, i ^ 3) for i in range(shards)])
    coefs = coef_call(picks, live, momentum, grad)
    squares, coefs = lax.optimization_barrier((squares, coefs))
    pack_m, pack_g, rest_m, rest_g = coefs

    mean = squares[0, :1] / float(rows * cols * shards)
    factor = jnp.minimum(1.0, 1.0 / jnp.sqrt(mean + 1e-06))
    own_steps = steps.astype(F32)
    payload = (0.9 * pack_m + factor * pack_g) * own_steps
    meta = jnp.concatenate([picks.astype(F32), own_steps, jnp.zeros((111,), F32)])
    sent = jnp.concatenate([payload.reshape(1, PAY), meta[None]], 1)
    sent = jnp.broadcast_to(sent[None], (half, 1, PAY + 128))
    got = lax.all_to_all(sent, "island", 0, 0, tiled=True, axis_index_groups=same_core)
    swapped = lax.ppermute(got, "island", other_core)

    momentum_next = (rest_m + factor * rest_g).astype(BF)
    first, first_steps = scatter_call(got, rows, cols)
    update = merge_call(swapped, first, first_steps, rows, cols)
    return (update, momentum_next[None], acts_grad)


def solution(mesh):
    placed = (
        P("shard", None),
        P("shard", "island"),
        P("island", None),
        P("island", "shard", None),
        P("island", "shard"),
        P("island", "shard"),
        P("island"),
    )
    return jax.shard_map(
        on_device,
        mesh=mesh,
        in_specs=placed,
        out_specs=(P("shard", None), P("island", "shard", None), P("shard", "island")),
        check_vma=False,
    )
```

```python
import functools

import jax
import jax.numpy as jnp
import ml_dtypes
import numpy as np
from jax import lax
from jax.experimental import pallas as pl
from jax.experimental.pallas import tpu as pltpu
from jax.sharding import PartitionSpec as P

BF = jnp.bfloat16
F32 = jnp.float32
SLOTS = 16
PAY = SLOTS * 128
MIB = 1 << 20


def dct_matrix():
    freq = np.arange(64, dtype=np.float64)[:, None]
    place = np.arange(64, dtype=np.float64)[None, :]
    waves = np.cos(np.pi * (2.0 * place + 1.0) * freq / 128.0)
    return np.where(freq == 0.0, 0.125, np.sqrt(2.0 / 64.0)) * waves


def halves(a):
    hi = a.astype(ml_dtypes.bfloat16)
    lo = (a - hi.astype(np.float64)).astype(ml_dtypes.bfloat16)
    return hi, lo


COS = dct_matrix()
COS_HI, COS_LO = halves(COS)
INV_HI, INV_LO = halves(COS.T)


def diagonal(a, copies):
    return np.kron(np.eye(copies), a.astype(np.float64)).astype(ml_dtypes.bfloat16)


FWD_LEFT3 = np.concatenate([COS_HI, COS_HI, COS_LO], 1)
FWD_LEFT2 = np.concatenate([COS_HI, COS_LO], 1)
INV_LEFT3 = np.concatenate([INV_HI, INV_HI, INV_LO], 1)
FWD_RIGHT3 = np.concatenate([diagonal(COS_HI.T, 2), diagonal(COS_HI.T, 2), diagonal(COS_LO.T, 2)], 0)
INV_RIGHT3 = np.concatenate([diagonal(COS_HI, 2), diagonal(COS_HI, 2), diagonal(COS_LO, 2)], 0)
INV_RIGHT2 = np.block([
    [diagonal(COS_HI, 2), diagonal(COS_LO, 2)],
    [diagonal(COS_HI, 2), np.zeros((128, 128), ml_dtypes.bfloat16)],
])


def split(x):
    hi = x.astype(BF)
    return hi, (x - hi.astype(F32)).astype(BF)


def dot(a, b):
    return jnp.dot(a, b, preferred_element_type=F32)


PARTS = 2


def grad_kernel(acts, og, weight, grad, squares, og_in, weight_in, acts_in, sem):
    cols = og_in.shape[1]
    width = cols // PARTS
    first = pltpu.make_async_copy(acts, acts_in, sem.at[PARTS])
    first.start()
    parts = []
    for i in range(PARTS):
        at = slice(i * width, (i + 1) * width)
        parts.append(pltpu.make_async_copy(og.at[:, at], og_in.at[:, at], sem.at[i]))
        parts[i].start()
    last = pltpu.make_async_copy(weight, weight_in, sem.at[PARTS + 1])
    last.start()
    first.wait()
    a = acts_in[...]
    total = jnp.zeros((8, 512), F32)
    for i in range(PARTS):
        at = slice(i * width, (i + 1) * width)
        parts[i].wait()
        g = dot(a, og_in[:, at])
        grad[:, at] = g
        g = jnp.sum((g * g).reshape(-1, 8, width), axis=0)
        for k in range(0, width, 512):
            total = total + g[:, k:k + 512]
    squares[...] = jnp.full(squares.shape, jnp.sum(total), F32)
    last.wait()


def grad_call(acts, og, weight):
    rows, toks = acts.shape
    cols = og.shape[1]
    vm = pl.BlockSpec(memory_space=pltpu.VMEM)
    anyw = pl.BlockSpec(memory_space=pl.ANY)
    held = [pltpu.with_memory_space_constraint(x, pltpu.HBM) for x in (acts, og, weight)]
    return pl.pallas_call(
        grad_kernel,
        in_specs=[anyw] * 3,
        out_specs=[vm] * 4,
        out_shape=[
            jax.ShapeDtypeStruct((rows, cols), F32),
            jax.ShapeDtypeStruct((1, 128), F32),
            jax.ShapeDtypeStruct((toks, cols), BF),
            jax.ShapeDtypeStruct((rows, cols), BF),
        ],
        scratch_shapes=[
            pltpu.VMEM((rows, toks), BF),
            pltpu.SemaphoreType.DMA((PARTS + 2,)),
        ],
        compiler_params=pltpu.CompilerParams(vmem_limit_bytes=24 * MIB),
        cost_estimate=pl.CostEstimate(flops=2 * rows * toks * cols, bytes_accessed=6 * MIB, transcendentals=0),
        name="weight_grad",
    )(*held)


def acts_grad_kernel(weight, og, out):
    total = lax.dot_general(og[...], weight[...], (((1,), (1,)), ((), ())), preferred_element_type=F32)
    out[...] = total.T.astype(BF)


def acts_grad_call(weight, og):
    rows, cols = weight.shape
    toks = og.shape[0]
    vm = pl.BlockSpec(memory_space=pltpu.VMEM)
    return pl.pallas_call(
        acts_grad_kernel,
        in_specs=[vm, vm],
        out_specs=vm,
        out_shape=jax.ShapeDtypeStruct((rows, toks), BF),
        compiler_params=pltpu.CompilerParams(vmem_limit_bytes=16 * MIB),
        cost_estimate=pl.CostEstimate(flops=2 * rows * toks * cols, bytes_accessed=5 * MIB, transcendentals=0),
        name="acts_grad",
    )(weight, og)


def lane_group(shape):
    return lax.broadcasted_iota(jnp.int32, shape, 1) >> 4


def coef_kernel(picks, counts, momentum, grad, left2, left3, right3, back_left3, back_right3,
                pack_m, pack_g, rest_m, rest_g,
                mom_in, grad_in, side_m, side_g, low, wide):
    pairs = [(picks[j] >> 3) & 63 for j in range(SLOTS)]
    lanes = [pl.ds(pl.multiple_of(p * 128, 128), 128) for p in pairs]
    tops = [pl.ds(pl.multiple_of((picks[j] >> 9) * 8, 8), 8) for j in range(SLOTS)]
    offs = [picks[j] & 7 for j in range(SLOTS)]
    here = [slice(128 * j, 128 * j + 128) for j in range(SLOTS)]
    for j in range(SLOTS):
        mom_in[:, here[j]] = momentum[:, lanes[j]]
        grad_in[:, here[j]] = grad[:, lanes[j]]
    wide[...] = jnp.zeros_like(wide)
    m = mom_in[...]
    g_hi, g_lo = split(grad_in[...])
    side_m[...] = dot(left2[...], jnp.concatenate([m, m], 0))
    side_g[...] = dot(left3[...], jnp.concatenate([g_hi, g_lo, g_hi], 0))
    for j in range(SLOTS):
        low[8 * j:8 * j + 8, :] = side_m[tops[j], here[j]]
        low[128 + 8 * j:136 + 8 * j, :] = side_g[tops[j], here[j]]
    hi, lo = split(low[...])
    low[...] = dot(jnp.concatenate([hi, lo, hi], 1), right3[...])
    group = lane_group((8, 128))
    live = counts[0]
    wants = [jnp.where(j < live, offs[j], 8) for j in range(SLOTS)]
    for base, pack in ((0, pack_m), (128, pack_g)):
        packed = [jnp.zeros((8, 128), F32)] * 2
        for j in range(SLOTS):
            at = slice(base + 8 * j, base + 8 * j + 8)
            kept = jnp.where(group == wants[j], low[at, :], 0.0)
            low[at, :] = kept
            packed[j // 8] = packed[j // 8] + pltpu.roll(kept, ((j % 8 - offs[j]) & 7) * 16, 1)
        pack[0:8, :] = packed[0]
        pack[8:16, :] = packed[1]
    hi, lo = split(low[...])
    low[...] = dot(jnp.concatenate([hi, lo, hi], 1), back_right3[...])
    for j in range(SLOTS):
        wide[tops[j], 128 * j:128 * j + 128] = low[8 * j:8 * j + 8, :]
        wide[tops[j], PAY + 128 * j:PAY + 128 * j + 128] = low[128 + 8 * j:136 + 8 * j, :]
    hi, lo = split(wide[...])
    wide[...] = dot(back_left3[...], jnp.concatenate([hi, lo, hi], 0))
    cols = grad.shape[1]
    for c in range(0, cols, 1024):
        at = slice(c, c + 1024)
        rest_m[:, at] = 0.9 * momentum[:, at].astype(F32)
        rest_g[:, at] = grad[:, at]
    for j in range(SLOTS):
        rest_m[:, lanes[j]] = rest_m[:, lanes[j]] - 0.9 * wide[:, 128 * j:128 * j + 128]
        rest_g[:, lanes[j]] = rest_g[:, lanes[j]] - wide[:, PAY + 128 * j:PAY + 128 * j + 128]


def coef_call(picks, counts, momentum, grad):
    rows, cols = grad.shape
    vm = pl.BlockSpec(memory_space=pltpu.VMEM)
    sm = pl.BlockSpec(memory_space=pltpu.SMEM)
    return pl.pallas_call(
        coef_kernel,
        in_specs=[sm, sm] + [vm] * 7,
        out_specs=[vm] * 4,
        out_shape=[
            jax.ShapeDtypeStruct((16, 128), F32),
            jax.ShapeDtypeStruct((16, 128), F32),
            jax.ShapeDtypeStruct((rows, cols), F32),
            jax.ShapeDtypeStruct((rows, cols), F32),
        ],
        scratch_shapes=[
            pltpu.VMEM((rows, PAY), BF),
            pltpu.VMEM((rows, PAY), F32),
            pltpu.VMEM((rows, PAY), F32),
            pltpu.VMEM((rows, PAY), F32),
            pltpu.VMEM((256, 128), F32),
            pltpu.VMEM((rows, 2 * PAY), F32),
        ],
        compiler_params=pltpu.CompilerParams(vmem_limit_bytes=24 * MIB),
        cost_estimate=pl.CostEstimate(flops=300_000_000, bytes_accessed=8 * MIB, transcendentals=0),
        name="selected_coefs",
    )(picks, counts, momentum, grad, FWD_LEFT2, FWD_LEFT3, FWD_RIGHT3, INV_LEFT3, INV_RIGHT3)


GROUP = 8
SHARE = 4


def gather_meta(got, ints, picks, sem):
    rows = []
    for a in range(got.shape[0] // SHARE):
        turned = [got[SHARE * a + k, :, PAY:] for k in range(SHARE)]
        turned = [turned[0]] + [pltpu.roll(turned[k], 32 * k, 1) for k in range(1, SHARE)]
        rows.append(sum(turned))
    rows = jnp.concatenate(rows, 0)
    ints[...] = rows.astype(jnp.int32)
    to_scalars = pltpu.make_async_copy(ints, picks, sem)
    to_scalars.start()
    lane = lax.broadcasted_iota(jnp.int32, rows.shape, 1)
    return to_scalars, jnp.sum(jnp.where((lane & 31) == SLOTS, rows, 0.0))


def add_islands(got, grid, picks):
    group = lane_group((8, 128))

    def some(a, carry):
        for k in range(SHARE):
            i = SHARE * a + k
            tiles = [got[i, 0, 1024 * t:1024 * t + 1024].reshape(8, 128) for t in range(2)]
            olds, news, masks, places = [], [], [], []
            for j in range(SLOTS):
                b = picks[a, 32 * k + j]
                off = b & 7
                place = b >> 3
                news.append(pltpu.roll(tiles[j // 8], ((off - j % 8) & 7) * 16, 1))
                olds.append(grid[place])
                masks.append(group == off)
                places.append(place)
            for j in range(SLOTS):
                pltpu.store(grid.at[places[j]], olds[j] + news[j], mask=masks[j])
        return carry

    lax.fori_loop(0, got.shape[0] // SHARE, some, 0)


def scatter_kernel(got, factor, rest_m, rest_g, grid, steps, rest, ints, picks, rest_out, sem, out_sem):
    to_scalars, total = gather_meta(got, ints, picks, sem)
    steps[...] = jnp.full(steps.shape, total, F32)
    grid[...] = jnp.zeros_like(grid)
    f = factor[:, :1]
    cols = rest_out.shape[1]
    width = cols // 4
    copies = []
    for q in range(4):
        at = slice(width * q, width * q + width)
        rest_out[:, at] = (rest_m[:, at] + f * rest_g[:, at]).astype(BF)
        copies.append(pltpu.make_async_copy(rest_out.at[:, at], rest.at[:, at], out_sem.at[q]))
        copies[q].start()
    to_scalars.wait()
    add_islands(got, grid, picks)
    for c in copies:
        c.wait()


def scatter_call(got, factor, rest_m, rest_g):
    rows, cols = rest_m.shape
    vm = pl.BlockSpec(memory_space=pltpu.VMEM)
    islands = got.shape[0]
    return pl.pallas_call(
        scatter_kernel,
        in_specs=[vm] * 4,
        out_specs=[vm, vm, pl.BlockSpec(memory_space=pl.ANY)],
        out_shape=[
            jax.ShapeDtypeStruct((rows * cols // 1024, 8, 128), F32),
            jax.ShapeDtypeStruct((1, 128), F32),
            jax.ShapeDtypeStruct((rows, cols), BF),
        ],
        scratch_shapes=[
            pltpu.VMEM((islands // SHARE, 128), jnp.int32),
            pltpu.SMEM((islands // SHARE, 128), jnp.int32),
            pltpu.VMEM((rows, cols), BF),
            pltpu.SemaphoreType.DMA,
            pltpu.SemaphoreType.DMA((4,)),
        ],
        compiler_params=pltpu.CompilerParams(vmem_limit_bytes=16 * MIB),
        cost_estimate=pl.CostEstimate(flops=300_000_000, bytes_accessed=8 * MIB, transcendentals=0),
        name="scatter_own",
    )(got, factor, rest_m, rest_g)


def merge_kernel(got, first, first_steps, left3, right2, out, grid, ints, picks, done, sem, out_sem):
    to_scalars, total = gather_meta(got, ints, picks, sem)
    grid[...] = jnp.zeros_like(grid)
    s = 2.0 * got.shape[0] / (total + first_steps[0, 0])
    to_scalars.wait()
    add_islands(got, grid, picks)
    pairs = grid.shape[0] // 8
    width = 256 * GROUP
    copies = []
    for q in range(pairs // (2 * GROUP)):
        parts = []
        for k in range(2 * GROUP):
            at = [r * pairs + 2 * GROUP * q + k for r in range(8)]
            parts.append(jnp.concatenate([grid[p] + first[p] for p in at], 0))
        hi, lo = split(jnp.concatenate(parts, 1))
        z = dot(left3[...], jnp.concatenate([hi, lo, hi], 0)) * s
        z = jnp.concatenate([z[:, 128 * k:128 * k + 128] for k in range(2 * GROUP)], 0)
        hi, lo = split(z)
        y = dot(jnp.concatenate([hi, lo], 1), right2[...])
        y = (y[:, :128] + y[:, 128:]).astype(BF)
        for k in range(2 * GROUP):
            at = width * q + 128 * k
            done[:, at:at + 128] = y[64 * k:64 * k + 64]
        at = slice(width * q, width * q + width)
        copies.append(pltpu.make_async_copy(done.at[:, at], out.at[:, at], out_sem.at[q]))
        copies[q].start()
    for c in copies:
        c.wait()


def merge_call(got, first, first_steps, rows, cols):
    vm = pl.BlockSpec(memory_space=pltpu.VMEM)
    anyw = pl.BlockSpec(memory_space=pl.ANY)
    islands = got.shape[0]
    return pl.pallas_call(
        merge_kernel,
        in_specs=[vm] * 5,
        out_specs=anyw,
        out_shape=jax.ShapeDtypeStruct((rows, cols), BF),
        scratch_shapes=[
            pltpu.VMEM((rows * cols // 1024, 8, 128), F32),
            pltpu.VMEM((islands // SHARE, 128), jnp.int32),
            pltpu.SMEM((islands // SHARE, 128), jnp.int32),
            pltpu.VMEM((rows, cols), BF),
            pltpu.SemaphoreType.DMA,
            pltpu.SemaphoreType.DMA((cols // (256 * GROUP),)),
        ],
        compiler_params=pltpu.CompilerParams(vmem_limit_bytes=32 * MIB),
        cost_estimate=pl.CostEstimate(flops=1_000_000_000, bytes_accessed=2 * MIB, transcendentals=0),
        name="merge_update",
    )(got, first, first_steps, INV_LEFT3, INV_RIGHT2)


def on_device(weight, acts_t, out_grad, momentum, chosen, counts, steps):
    rows, cols = weight.shape
    islands = lax.axis_size("island")
    shards = lax.axis_size("shard")
    half = islands // 2
    same_core = [[2 * i + c for i in range(half)] for c in range(2)]
    other_core = [(i, i ^ 1) for i in range(islands)]
    momentum = momentum[0]

    grad, squares, og_held, weight_held = grad_call(acts_t, out_grad, weight)
    grad, og_held, weight_held = [
        pltpu.with_memory_space_constraint(x, pltpu.VMEM) for x in (grad, og_held, weight_held)
    ]
    squares = squares + lax.ppermute(squares, "shard", [(i, i ^ 1) for i in range(shards)])
    acts_grad = acts_grad_call(weight_held, og_held)
    squares, acts_grad = lax.optimization_barrier((squares, acts_grad))
    squares = squares + lax.ppermute(squares, "shard", [(i, i ^ 3) for i in range(shards)])
    picks = chosen[0] % (rows * cols // 128)
    own_steps = steps.astype(F32)
    meta = jnp.concatenate([picks.astype(F32), own_steps, jnp.zeros((111,), F32)])
    coefs = coef_call(picks, counts[0], momentum, grad)
    squares, coefs, meta = lax.optimization_barrier((squares, coefs, meta))
    pack_m, pack_g, rest_m, rest_g = coefs

    mean = squares / float(rows * cols * shards)
    factor = jnp.minimum(1.0, 1.0 / jnp.sqrt(mean + 1e-06))
    payload = (0.9 * pack_m + factor * pack_g) * own_steps
    sent = jnp.concatenate([payload.reshape(1, PAY), meta[None]], 1)
    sent = jnp.broadcast_to(sent[None], (half, 1, PAY + 128))
    got = lax.all_to_all(sent, "island", 0, 0, tiled=True, axis_index_groups=same_core)
    swapped = lax.ppermute(got, "island", other_core)

    first, first_steps, momentum_next = scatter_call(got, factor, rest_m, rest_g)
    update = merge_call(swapped, first, first_steps, rows, cols)
    return (update, momentum_next[None], acts_grad)


def solution(mesh):
    placed = (
        P("shard", None),
        P("shard", "island"),
        P("island", None),
        P("island", "shard", None),
        P("island", "shard"),
        P("island", "shard"),
        P("island"),
    )
    return jax.shard_map(
        on_device,
        mesh=mesh,
        in_specs=placed,
        out_specs=(P("shard", None), P("island", "shard", None), P("shard", "island")),
        check_vma=False,
    )
```

```python
import functools

import jax
import jax.numpy as jnp
import ml_dtypes
import numpy as np
from jax import lax
from jax.experimental import pallas as pl
from jax.experimental.pallas import tpu as pltpu
from jax.sharding import PartitionSpec as P

BF = jnp.bfloat16
F32 = jnp.float32
SLOTS = 16
PAY = SLOTS * 128
MIB = 1 << 20


def dct_matrix():
    freq = np.arange(64, dtype=np.float64)[:, None]
    place = np.arange(64, dtype=np.float64)[None, :]
    waves = np.cos(np.pi * (2.0 * place + 1.0) * freq / 128.0)
    return np.where(freq == 0.0, 0.125, np.sqrt(2.0 / 64.0)) * waves


def halves(a):
    hi = a.astype(ml_dtypes.bfloat16)
    lo = (a - hi.astype(np.float64)).astype(ml_dtypes.bfloat16)
    return hi, lo


COS = dct_matrix()
COS_HI, COS_LO = halves(COS)
INV_HI, INV_LO = halves(COS.T)


def diagonal(a, copies):
    return np.kron(np.eye(copies), a.astype(np.float64)).astype(ml_dtypes.bfloat16)


FWD_LEFT3 = np.concatenate([COS_HI, COS_HI, COS_LO], 1)
FWD_LEFT2 = np.concatenate([COS_HI, COS_LO], 1)
INV_LEFT3 = np.concatenate([INV_HI, INV_HI, INV_LO], 1)
MIRROR = np.array([8 * r + (8 - u) % 8 for r in range(8) for u in range(8)])
INV_LEFT3_MIRROR = np.concatenate([INV_HI[:, MIRROR], INV_HI[:, MIRROR], INV_LO[:, MIRROR]], 1)
FWD_RIGHT3 = np.concatenate([diagonal(COS_HI.T, 2), diagonal(COS_HI.T, 2), diagonal(COS_LO.T, 2)], 0)
INV_RIGHT3 = np.concatenate([diagonal(COS_HI, 2), diagonal(COS_HI, 2), diagonal(COS_LO, 2)], 0)
INV_RIGHT2 = np.block([
    [diagonal(COS_HI, 2), diagonal(COS_LO, 2)],
    [diagonal(COS_HI, 2), np.zeros((128, 128), ml_dtypes.bfloat16)],
])


def split(x):
    hi = x.astype(BF)
    return hi, (x - hi.astype(F32)).astype(BF)


def dot(a, b):
    return jnp.dot(a, b, preferred_element_type=F32)


PARTS = 2


def grad_kernel(acts, og, weight, grad, squares, og_in, weight_in, acts_in, sem):
    cols = og_in.shape[1]
    width = cols // PARTS
    first = pltpu.make_async_copy(acts, acts_in, sem.at[PARTS])
    first.start()
    parts = []
    for i in range(PARTS):
        at = slice(i * width, (i + 1) * width)
        parts.append(pltpu.make_async_copy(og.at[:, at], og_in.at[:, at], sem.at[i]))
        parts[i].start()
    last = pltpu.make_async_copy(weight, weight_in, sem.at[PARTS + 1])
    last.start()
    first.wait()
    a = acts_in[...]
    total = jnp.zeros((8, 512), F32)
    for i in range(PARTS):
        at = slice(i * width, (i + 1) * width)
        parts[i].wait()
        g = dot(a, og_in[:, at])
        grad[:, at] = g
        g = jnp.sum((g * g).reshape(-1, 8, width), axis=0)
        for k in range(0, width, 512):
            total = total + g[:, k:k + 512]
    squares[...] = jnp.full(squares.shape, jnp.sum(total), F32)
    last.wait()


def grad_call(acts, og, weight):
    rows, toks = acts.shape
    cols = og.shape[1]
    vm = pl.BlockSpec(memory_space=pltpu.VMEM)
    anyw = pl.BlockSpec(memory_space=pl.ANY)
    held = [pltpu.with_memory_space_constraint(x, pltpu.HBM) for x in (acts, og, weight)]
    return pl.pallas_call(
        grad_kernel,
        in_specs=[anyw] * 3,
        out_specs=[vm] * 4,
        out_shape=[
            jax.ShapeDtypeStruct((rows, cols), F32),
            jax.ShapeDtypeStruct((1, 128), F32),
            jax.ShapeDtypeStruct((toks, cols), BF),
            jax.ShapeDtypeStruct((rows, cols), BF),
        ],
        scratch_shapes=[
            pltpu.VMEM((rows, toks), BF),
            pltpu.SemaphoreType.DMA((PARTS + 2,)),
        ],
        compiler_params=pltpu.CompilerParams(vmem_limit_bytes=24 * MIB),
        cost_estimate=pl.CostEstimate(flops=2 * rows * toks * cols, bytes_accessed=6 * MIB, transcendentals=0),
        name="weight_grad",
    )(*held)


def acts_grad_kernel(weight, og, out):
    total = lax.dot_general(og[...], weight[...], (((1,), (1,)), ((), ())), preferred_element_type=F32)
    out[...] = total.T.astype(BF)


def acts_grad_call(weight, og):
    rows, cols = weight.shape
    toks = og.shape[0]
    vm = pl.BlockSpec(memory_space=pltpu.VMEM)
    return pl.pallas_call(
        acts_grad_kernel,
        in_specs=[vm, vm],
        out_specs=vm,
        out_shape=jax.ShapeDtypeStruct((rows, toks), BF),
        compiler_params=pltpu.CompilerParams(vmem_limit_bytes=16 * MIB),
        cost_estimate=pl.CostEstimate(flops=2 * rows * toks * cols, bytes_accessed=5 * MIB, transcendentals=0),
        name="acts_grad",
    )(weight, og)


def lane_group(shape):
    return lax.broadcasted_iota(jnp.int32, shape, 1) >> 4


def coef_kernel(picks, counts, momentum, grad, left2, left3, right3, back_left3, back_right3,
                pack_m, pack_g, rest_m, rest_g,
                mom_in, grad_in, side_m, side_g, low, wide):
    pairs = [(picks[j] >> 3) & 63 for j in range(SLOTS)]
    lanes = [pl.ds(pl.multiple_of(p * 128, 128), 128) for p in pairs]
    tops = [pl.ds(pl.multiple_of((picks[j] >> 9) * 8, 8), 8) for j in range(SLOTS)]
    offs = [picks[j] & 7 for j in range(SLOTS)]
    here = [slice(128 * j, 128 * j + 128) for j in range(SLOTS)]
    for j in range(SLOTS):
        mom_in[:, here[j]] = momentum[:, lanes[j]]
        grad_in[:, here[j]] = grad[:, lanes[j]]
    wide[...] = jnp.zeros_like(wide)
    m = mom_in[...]
    g_hi, g_lo = split(grad_in[...])
    side_m[...] = dot(left2[...], jnp.concatenate([m, m], 0))
    side_g[...] = dot(left3[...], jnp.concatenate([g_hi, g_lo, g_hi], 0))
    for j in range(SLOTS):
        low[8 * j:8 * j + 8, :] = side_m[tops[j], here[j]]
        low[128 + 8 * j:136 + 8 * j, :] = side_g[tops[j], here[j]]
    hi, lo = split(low[...])
    low[...] = dot(jnp.concatenate([hi, lo, hi], 1), right3[...])
    group = lane_group((8, 128))
    live = counts[0]
    wants = [jnp.where(j < live, offs[j], 8) for j in range(SLOTS)]
    for base, pack in ((0, pack_m), (128, pack_g)):
        for j in range(SLOTS):
            at = slice(base + 8 * j, base + 8 * j + 8)
            kept = jnp.where(group == wants[j], low[at, :], 0.0)
            low[at, :] = kept
            turned = pltpu.roll(kept, 0, 1, stride=16, stride_axis=0)
            pack[j:j + 1, :] = jnp.sum(turned, axis=0, keepdims=True)
    hi, lo = split(low[...])
    low[...] = dot(jnp.concatenate([hi, lo, hi], 1), back_right3[...])
    for j in range(SLOTS):
        wide[tops[j], 128 * j:128 * j + 128] = low[8 * j:8 * j + 8, :]
        wide[tops[j], PAY + 128 * j:PAY + 128 * j + 128] = low[128 + 8 * j:136 + 8 * j, :]
    hi, lo = split(wide[...])
    wide[...] = dot(back_left3[...], jnp.concatenate([hi, lo, hi], 0))
    cols = grad.shape[1]
    for c in range(0, cols, 1024):
        at = slice(c, c + 1024)
        rest_m[:, at] = 0.9 * momentum[:, at].astype(F32)
        rest_g[:, at] = grad[:, at]
    for j in range(SLOTS):
        rest_m[:, lanes[j]] = rest_m[:, lanes[j]] - 0.9 * wide[:, 128 * j:128 * j + 128]
        rest_g[:, lanes[j]] = rest_g[:, lanes[j]] - wide[:, PAY + 128 * j:PAY + 128 * j + 128]


def coef_call(picks, counts, momentum, grad):
    rows, cols = grad.shape
    vm = pl.BlockSpec(memory_space=pltpu.VMEM)
    sm = pl.BlockSpec(memory_space=pltpu.SMEM)
    return pl.pallas_call(
        coef_kernel,
        in_specs=[sm, sm] + [vm] * 7,
        out_specs=[vm] * 4,
        out_shape=[
            jax.ShapeDtypeStruct((16, 128), F32),
            jax.ShapeDtypeStruct((16, 128), F32),
            jax.ShapeDtypeStruct((rows, cols), F32),
            jax.ShapeDtypeStruct((rows, cols), F32),
        ],
        scratch_shapes=[
            pltpu.VMEM((rows, PAY), BF),
            pltpu.VMEM((rows, PAY), F32),
            pltpu.VMEM((rows, PAY), F32),
            pltpu.VMEM((rows, PAY), F32),
            pltpu.VMEM((256, 128), F32),
            pltpu.VMEM((rows, 2 * PAY), F32),
        ],
        compiler_params=pltpu.CompilerParams(vmem_limit_bytes=24 * MIB),
        cost_estimate=pl.CostEstimate(flops=300_000_000, bytes_accessed=8 * MIB, transcendentals=0),
        name="selected_coefs",
    )(picks, counts, momentum, grad, FWD_LEFT2, FWD_LEFT3, FWD_RIGHT3, INV_LEFT3, INV_RIGHT3)


GROUP = 8
SHARE = 4


def gather_meta(got, ints, picks, sem):
    rows = []
    for a in range(got.shape[0] // SHARE):
        turned = [got[SHARE * a + k, :, PAY:] for k in range(SHARE)]
        turned = [turned[0]] + [pltpu.roll(turned[k], 32 * k, 1) for k in range(1, SHARE)]
        rows.append(sum(turned))
    rows = jnp.concatenate(rows, 0)
    ints[...] = rows.astype(jnp.int32)
    to_scalars = pltpu.make_async_copy(ints, picks, sem)
    to_scalars.start()
    lane = lax.broadcasted_iota(jnp.int32, rows.shape, 1)
    return to_scalars, jnp.sum(jnp.where((lane & 31) == SLOTS, rows, 0.0))


def add_islands(got, grid, picks):
    def some(a, carry):
        for k in range(SHARE):
            i = SHARE * a + k
            places = [pl.ds(pl.multiple_of(picks[a, 32 * k + j] * 128, 128), 128) for j in range(SLOTS)]
            sums = [grid[0, places[j]] + got[i, 0, 128 * j:128 * j + 128] for j in range(SLOTS)]
            for j in range(SLOTS):
                grid[0, places[j]] = sums[j]
        return carry

    lax.fori_loop(0, got.shape[0] // SHARE, some, 0)


def untwist(x, group):
    for k in range(3):
        x = jnp.where((group & (1 << k)) != 0, pltpu.roll(x, 8 - (1 << k), 0), x)
    return pltpu.roll(x, 0, 1, stride=16, stride_axis=0)


def scatter_kernel(got, factor, rest_m, rest_g, grid, steps, rest, ints, picks, rest_out, sem, out_sem):
    to_scalars, total = gather_meta(got, ints, picks, sem)
    steps[...] = jnp.full(steps.shape, total, F32)
    grid[...] = jnp.zeros_like(grid)
    f = factor[:, :1]
    cols = rest_out.shape[1]
    width = cols // 4
    copies = []
    for q in range(4):
        at = slice(width * q, width * q + width)
        rest_out[:, at] = (rest_m[:, at] + f * rest_g[:, at]).astype(BF)
        copies.append(pltpu.make_async_copy(rest_out.at[:, at], rest.at[:, at], out_sem.at[q]))
        copies[q].start()
    to_scalars.wait()
    add_islands(got, grid, picks)
    for c in copies:
        c.wait()


def scatter_call(got, factor, rest_m, rest_g):
    rows, cols = rest_m.shape
    vm = pl.BlockSpec(memory_space=pltpu.VMEM)
    islands = got.shape[0]
    return pl.pallas_call(
        scatter_kernel,
        in_specs=[vm] * 4,
        out_specs=[vm, vm, pl.BlockSpec(memory_space=pl.ANY)],
        out_shape=[
            jax.ShapeDtypeStruct((1, rows * cols), F32),
            jax.ShapeDtypeStruct((1, 128), F32),
            jax.ShapeDtypeStruct((rows, cols), BF),
        ],
        scratch_shapes=[
            pltpu.VMEM((islands // SHARE, 128), jnp.int32),
            pltpu.SMEM((islands // SHARE, 128), jnp.int32),
            pltpu.VMEM((rows, cols), BF),
            pltpu.SemaphoreType.DMA,
            pltpu.SemaphoreType.DMA((4,)),
        ],
        compiler_params=pltpu.CompilerParams(vmem_limit_bytes=16 * MIB),
        cost_estimate=pl.CostEstimate(flops=300_000_000, bytes_accessed=8 * MIB, transcendentals=0),
        name="scatter_own",
    )(got, factor, rest_m, rest_g)


def merge_kernel(got, first, first_steps, left3, right2, out, grid, ints, picks, done, sem, out_sem):
    to_scalars, total = gather_meta(got, ints, picks, sem)
    grid[...] = jnp.zeros_like(grid)
    s = 2.0 * got.shape[0] / (total + first_steps[0, 0])
    to_scalars.wait()
    add_islands(got, grid, picks)
    pairs = grid.shape[1] // 8192
    width = 256 * GROUP
    group = lane_group((8, 128))
    copies = []
    for q in range(pairs // (2 * GROUP)):
        parts = []
        for k in range(2 * GROUP):
            tiles = []
            for r in range(8):
                at = 1024 * (r * pairs + 2 * GROUP * q + k)
                tile = (grid[0, at:at + 1024] + first[0, at:at + 1024]).reshape(8, 128)
                tiles.append(untwist(tile, group))
            parts.append(jnp.concatenate(tiles, 0))
        hi, lo = split(jnp.concatenate(parts, 1))
        z = dot(left3[...], jnp.concatenate([hi, lo, hi], 0)) * s
        z = jnp.concatenate([z[:, 128 * k:128 * k + 128] for k in range(2 * GROUP)], 0)
        hi, lo = split(z)
        y = dot(jnp.concatenate([hi, lo], 1), right2[...])
        y = (y[:, :128] + y[:, 128:]).astype(BF)
        for k in range(2 * GROUP):
            at = width * q + 128 * k
            done[:, at:at + 128] = y[64 * k:64 * k + 64]
        at = slice(width * q, width * q + width)
        copies.append(pltpu.make_async_copy(done.at[:, at], out.at[:, at], out_sem.at[q]))
        copies[q].start()
    for c in copies:
        c.wait()


def merge_call(got, first, first_steps, rows, cols):
    vm = pl.BlockSpec(memory_space=pltpu.VMEM)
    anyw = pl.BlockSpec(memory_space=pl.ANY)
    islands = got.shape[0]
    return pl.pallas_call(
        merge_kernel,
        in_specs=[vm] * 5,
        out_specs=anyw,
        out_shape=jax.ShapeDtypeStruct((rows, cols), BF),
        scratch_shapes=[
            pltpu.VMEM((1, rows * cols), F32),
            pltpu.VMEM((islands // SHARE, 128), jnp.int32),
            pltpu.SMEM((islands // SHARE, 128), jnp.int32),
            pltpu.VMEM((rows, cols), BF),
            pltpu.SemaphoreType.DMA,
            pltpu.SemaphoreType.DMA((cols // (256 * GROUP),)),
        ],
        compiler_params=pltpu.CompilerParams(vmem_limit_bytes=32 * MIB),
        cost_estimate=pl.CostEstimate(flops=1_000_000_000, bytes_accessed=2 * MIB, transcendentals=0),
        name="merge_update",
    )(got, first, first_steps, INV_LEFT3_MIRROR, INV_RIGHT2)


def on_device(weight, acts_t, out_grad, momentum, chosen, counts, steps):
    rows, cols = weight.shape
    islands = lax.axis_size("island")
    shards = lax.axis_size("shard")
    half = islands // 2
    same_core = [[2 * i + c for i in range(half)] for c in range(2)]
    other_core = [(i, i ^ 1) for i in range(islands)]
    momentum = momentum[0]

    grad, squares, og_held, weight_held = grad_call(acts_t, out_grad, weight)
    grad, og_held, weight_held = [
        pltpu.with_memory_space_constraint(x, pltpu.VMEM) for x in (grad, og_held, weight_held)
    ]
    squares = squares + lax.ppermute(squares, "shard", [(i, i ^ 1) for i in range(shards)])
    acts_grad = acts_grad_call(weight_held, og_held)
    squares, acts_grad = lax.optimization_barrier((squares, acts_grad))
    squares = squares + lax.ppermute(squares, "shard", [(i, i ^ 3) for i in range(shards)])
    picks = chosen[0] % (rows * cols // 128)
    own_steps = steps.astype(F32)
    meta = jnp.concatenate([picks.astype(F32), own_steps, jnp.zeros((111,), F32)])
    coefs = coef_call(picks, counts[0], momentum, grad)
    squares, coefs, meta = lax.optimization_barrier((squares, coefs, meta))
    pack_m, pack_g, rest_m, rest_g = coefs

    mean = squares / float(rows * cols * shards)
    factor = jnp.minimum(1.0, 1.0 / jnp.sqrt(mean + 1e-06))
    payload = (0.9 * pack_m + factor * pack_g) * own_steps
    sent = jnp.concatenate([payload.reshape(1, PAY), meta[None]], 1)
    sent = jnp.broadcast_to(sent[None], (half, 1, PAY + 128))
    got = lax.all_to_all(sent, "island", 0, 0, tiled=True, axis_index_groups=same_core)
    swapped = lax.ppermute(got, "island", other_core)

    first, first_steps, momentum_next = scatter_call(got, factor, rest_m, rest_g)
    update = merge_call(swapped, first, first_steps, rows, cols)
    return (update, momentum_next[None], acts_grad)


def solution(mesh):
    placed = (
        P("shard", None),
        P("shard", "island"),
        P("island", None),
        P("island", "shard", None),
        P("island", "shard"),
        P("island", "shard"),
        P("island"),
    )
    return jax.shard_map(
        on_device,
        mesh=mesh,
        in_specs=placed,
        out_specs=(P("shard", None), P("island", "shard", None), P("shard", "island")),
        check_vma=False,
    )
```

```python
import functools

import jax
import jax.numpy as jnp
import ml_dtypes
import numpy as np
from jax import lax
from jax.experimental import pallas as pl
from jax.experimental.pallas import tpu as pltpu
from jax.sharding import PartitionSpec as P

BF = jnp.bfloat16
F32 = jnp.float32
SLOTS = 16
PAY = SLOTS * 128
MIB = 1 << 20


def dct_matrix():
    freq = np.arange(64, dtype=np.float64)[:, None]
    place = np.arange(64, dtype=np.float64)[None, :]
    waves = np.cos(np.pi * (2.0 * place + 1.0) * freq / 128.0)
    return np.where(freq == 0.0, 0.125, np.sqrt(2.0 / 64.0)) * waves


def halves(a):
    hi = a.astype(ml_dtypes.bfloat16)
    lo = (a - hi.astype(np.float64)).astype(ml_dtypes.bfloat16)
    return hi, lo


COS = dct_matrix()
COS_HI, COS_LO = halves(COS)
INV_HI, INV_LO = halves(COS.T)


def diagonal(a, copies):
    return np.kron(np.eye(copies), a.astype(np.float64)).astype(ml_dtypes.bfloat16)


FWD_LEFT3 = np.concatenate([COS_HI, COS_HI, COS_LO], 1)
FWD_LEFT2 = np.concatenate([COS_HI, COS_LO], 1)
INV_LEFT3 = np.concatenate([INV_HI, INV_HI, INV_LO], 1)
MIRROR = np.array([8 * r + (8 - u) % 8 for r in range(8) for u in range(8)])
INV_LEFT3_MIRROR = np.concatenate([INV_HI[:, MIRROR], INV_HI[:, MIRROR], INV_LO[:, MIRROR]], 1)
FWD_RIGHT3 = np.concatenate([diagonal(COS_HI.T, 2), diagonal(COS_HI.T, 2), diagonal(COS_LO.T, 2)], 0)
INV_RIGHT3 = np.concatenate([diagonal(COS_HI, 2), diagonal(COS_HI, 2), diagonal(COS_LO, 2)], 0)
INV_RIGHT2 = np.block([
    [diagonal(COS_HI, 2), diagonal(COS_LO, 2)],
    [diagonal(COS_HI, 2), np.zeros((128, 128), ml_dtypes.bfloat16)],
])


def split(x):
    hi = x.astype(BF)
    return hi, (x - hi.astype(F32)).astype(BF)


def dot(a, b):
    return jnp.dot(a, b, preferred_element_type=F32)


PARTS = 2


def grad_kernel(acts, og, weight, grad, squares, og_in, weight_in, acts_in, sem):
    cols = og_in.shape[1]
    width = cols // PARTS
    first = pltpu.make_async_copy(acts, acts_in, sem.at[PARTS])
    first.start()
    parts = []
    for i in range(PARTS):
        at = slice(i * width, (i + 1) * width)
        parts.append(pltpu.make_async_copy(og.at[:, at], og_in.at[:, at], sem.at[i]))
        parts[i].start()
    last = pltpu.make_async_copy(weight, weight_in, sem.at[PARTS + 1])
    last.start()
    first.wait()
    a = acts_in[...]
    total = jnp.zeros((8, 512), F32)
    for i in range(PARTS):
        at = slice(i * width, (i + 1) * width)
        parts[i].wait()
        g = dot(a, og_in[:, at])
        grad[:, at] = g
        g = jnp.sum((g * g).reshape(-1, 8, width), axis=0)
        for k in range(0, width, 512):
            total = total + g[:, k:k + 512]
    squares[...] = jnp.full(squares.shape, jnp.sum(total), F32)
    last.wait()


def grad_call(acts, og, weight):
    rows, toks = acts.shape
    cols = og.shape[1]
    vm = pl.BlockSpec(memory_space=pltpu.VMEM)
    anyw = pl.BlockSpec(memory_space=pl.ANY)
    held = [pltpu.with_memory_space_constraint(x, pltpu.HBM) for x in (acts, og, weight)]
    return pl.pallas_call(
        grad_kernel,
        in_specs=[anyw] * 3,
        out_specs=[vm] * 4,
        out_shape=[
            jax.ShapeDtypeStruct((rows, cols), F32),
            jax.ShapeDtypeStruct((1, 128), F32),
            jax.ShapeDtypeStruct((toks, cols), BF),
            jax.ShapeDtypeStruct((rows, cols), BF),
        ],
        scratch_shapes=[
            pltpu.VMEM((rows, toks), BF),
            pltpu.SemaphoreType.DMA((PARTS + 2,)),
        ],
        compiler_params=pltpu.CompilerParams(vmem_limit_bytes=24 * MIB),
        cost_estimate=pl.CostEstimate(flops=2 * rows * toks * cols, bytes_accessed=6 * MIB, transcendentals=0),
        name="weight_grad",
    )(*held)


def last_half():
    return lax.axis_index("island") >= lax.axis_size("island") // 2


def acts_product(weight, og):
    total = lax.dot_general(og, weight, (((1,), (1,)), ((), ())), preferred_element_type=F32)
    return total.T.astype(BF)


def acts_grad_kernel(weight, og, out):
    @pl.when(jnp.logical_not(last_half()))
    def _():
        out[...] = acts_product(weight[...], og[...])


def acts_grad_call(weight, og):
    rows, cols = weight.shape
    toks = og.shape[0]
    vm = pl.BlockSpec(memory_space=pltpu.VMEM)
    return pl.pallas_call(
        acts_grad_kernel,
        in_specs=[vm, vm],
        out_specs=vm,
        out_shape=jax.ShapeDtypeStruct((rows, toks), BF),
        compiler_params=pltpu.CompilerParams(vmem_limit_bytes=16 * MIB),
        cost_estimate=pl.CostEstimate(flops=2 * rows * toks * cols, bytes_accessed=5 * MIB, transcendentals=0),
        name="acts_grad",
    )(weight, og)


def lane_group(shape):
    return lax.broadcasted_iota(jnp.int32, shape, 1) >> 4


def coef_kernel(picks, counts, momentum, grad, left2, left3, right3, back_left3, back_right3,
                pack_m, pack_g, rest_m, rest_g,
                mom_in, grad_in, side_m, side_g, low, wide):
    pairs = [(picks[j] >> 3) & 63 for j in range(SLOTS)]
    lanes = [pl.ds(pl.multiple_of(p * 128, 128), 128) for p in pairs]
    tops = [pl.ds(pl.multiple_of((picks[j] >> 9) * 8, 8), 8) for j in range(SLOTS)]
    offs = [picks[j] & 7 for j in range(SLOTS)]
    here = [slice(128 * j, 128 * j + 128) for j in range(SLOTS)]
    for j in range(SLOTS):
        mom_in[:, here[j]] = momentum[:, lanes[j]]
        grad_in[:, here[j]] = grad[:, lanes[j]]
    wide[...] = jnp.zeros_like(wide)
    m = mom_in[...]
    g_hi, g_lo = split(grad_in[...])
    side_m[...] = dot(left2[...], jnp.concatenate([m, m], 0))
    side_g[...] = dot(left3[...], jnp.concatenate([g_hi, g_lo, g_hi], 0))
    for j in range(SLOTS):
        low[8 * j:8 * j + 8, :] = side_m[tops[j], here[j]]
        low[128 + 8 * j:136 + 8 * j, :] = side_g[tops[j], here[j]]
    hi, lo = split(low[...])
    low[...] = dot(jnp.concatenate([hi, lo, hi], 1), right3[...])
    group = lane_group((8, 128))
    live = counts[0]
    wants = [jnp.where(j < live, offs[j], 8) for j in range(SLOTS)]
    for base, pack in ((0, pack_m), (128, pack_g)):
        for j in range(SLOTS):
            at = slice(base + 8 * j, base + 8 * j + 8)
            kept = jnp.where(group == wants[j], low[at, :], 0.0)
            low[at, :] = kept
            turned = pltpu.roll(kept, 0, 1, stride=16, stride_axis=0)
            pack[j:j + 1, :] = jnp.sum(turned, axis=0, keepdims=True)
    hi, lo = split(low[...])
    low[...] = dot(jnp.concatenate([hi, lo, hi], 1), back_right3[...])
    for j in range(SLOTS):
        wide[tops[j], 128 * j:128 * j + 128] = low[8 * j:8 * j + 8, :]
        wide[tops[j], PAY + 128 * j:PAY + 128 * j + 128] = low[128 + 8 * j:136 + 8 * j, :]
    hi, lo = split(wide[...])
    wide[...] = dot(back_left3[...], jnp.concatenate([hi, lo, hi], 0))
    cols = grad.shape[1]
    for c in range(0, cols, 1024):
        at = slice(c, c + 1024)
        rest_m[:, at] = 0.9 * momentum[:, at].astype(F32)
        rest_g[:, at] = grad[:, at]
    for j in range(SLOTS):
        rest_m[:, lanes[j]] = rest_m[:, lanes[j]] - 0.9 * wide[:, 128 * j:128 * j + 128]
        rest_g[:, lanes[j]] = rest_g[:, lanes[j]] - wide[:, PAY + 128 * j:PAY + 128 * j + 128]


def coef_call(picks, counts, momentum, grad):
    rows, cols = grad.shape
    vm = pl.BlockSpec(memory_space=pltpu.VMEM)
    sm = pl.BlockSpec(memory_space=pltpu.SMEM)
    return pl.pallas_call(
        coef_kernel,
        in_specs=[sm, sm] + [vm] * 7,
        out_specs=[vm] * 4,
        out_shape=[
            jax.ShapeDtypeStruct((16, 128), F32),
            jax.ShapeDtypeStruct((16, 128), F32),
            jax.ShapeDtypeStruct((rows, cols), F32),
            jax.ShapeDtypeStruct((rows, cols), F32),
        ],
        scratch_shapes=[
            pltpu.VMEM((rows, PAY), BF),
            pltpu.VMEM((rows, PAY), F32),
            pltpu.VMEM((rows, PAY), F32),
            pltpu.VMEM((rows, PAY), F32),
            pltpu.VMEM((256, 128), F32),
            pltpu.VMEM((rows, 2 * PAY), F32),
        ],
        compiler_params=pltpu.CompilerParams(vmem_limit_bytes=24 * MIB),
        cost_estimate=pl.CostEstimate(flops=300_000_000, bytes_accessed=8 * MIB, transcendentals=0),
        name="selected_coefs",
    )(picks, counts, momentum, grad, FWD_LEFT2, FWD_LEFT3, FWD_RIGHT3, INV_LEFT3, INV_RIGHT3)


GROUP = 8
SHARE = 4


def gather_meta(got, ints, picks, sem):
    rows = []
    for a in range(got.shape[0] // SHARE):
        turned = [got[SHARE * a + k, :, PAY:] for k in range(SHARE)]
        turned = [turned[0]] + [pltpu.roll(turned[k], 32 * k, 1) for k in range(1, SHARE)]
        rows.append(sum(turned))
    rows = jnp.concatenate(rows, 0)
    ints[...] = rows.astype(jnp.int32)
    to_scalars = pltpu.make_async_copy(ints, picks, sem)
    to_scalars.start()
    lane = lax.broadcasted_iota(jnp.int32, rows.shape, 1)
    return to_scalars, jnp.sum(jnp.where((lane & 31) == SLOTS, rows, 0.0))


def add_islands(got, grid, picks):
    def some(a, carry):
        for k in range(SHARE):
            i = SHARE * a + k
            places = [pl.ds(pl.multiple_of(picks[a, 32 * k + j] * 128, 128), 128) for j in range(SLOTS)]
            sums = [grid[0, places[j]] + got[i, 0, 128 * j:128 * j + 128] for j in range(SLOTS)]
            for j in range(SLOTS):
                grid[0, places[j]] = sums[j]
        return carry

    lax.fori_loop(0, got.shape[0] // SHARE, some, 0, unroll=4)


def untwist(x, group):
    for k in range(3):
        x = jnp.where((group & (1 << k)) != 0, pltpu.roll(x, 8 - (1 << k), 0), x)
    return pltpu.roll(x, 0, 1, stride=16, stride_axis=0)


def scatter_kernel(got, factor, rest_m, rest_g, grid, steps, rest, ints, picks, rest_out, sem, out_sem):
    to_scalars, total = gather_meta(got, ints, picks, sem)
    steps[...] = jnp.full(steps.shape, total, F32)
    grid[...] = jnp.zeros_like(grid)
    f = factor[:, :1]
    cols = rest_out.shape[1]
    width = cols // 4
    copies = []
    for q in range(4):
        at = slice(width * q, width * q + width)
        rest_out[:, at] = (rest_m[:, at] + f * rest_g[:, at]).astype(BF)
        copies.append(pltpu.make_async_copy(rest_out.at[:, at], rest.at[:, at], out_sem.at[q]))
        copies[q].start()
    to_scalars.wait()
    add_islands(got, grid, picks)
    for c in copies:
        c.wait()


def scatter_call(got, factor, rest_m, rest_g):
    rows, cols = rest_m.shape
    vm = pl.BlockSpec(memory_space=pltpu.VMEM)
    islands = got.shape[0]
    return pl.pallas_call(
        scatter_kernel,
        in_specs=[vm] * 4,
        out_specs=[vm, vm, pl.BlockSpec(memory_space=pl.ANY)],
        out_shape=[
            jax.ShapeDtypeStruct((1, rows * cols), F32),
            jax.ShapeDtypeStruct((1, 128), F32),
            jax.ShapeDtypeStruct((rows, cols), BF),
        ],
        scratch_shapes=[
            pltpu.VMEM((islands // SHARE, 128), jnp.int32),
            pltpu.SMEM((islands // SHARE, 128), jnp.int32),
            pltpu.VMEM((rows, cols), BF),
            pltpu.SemaphoreType.DMA,
            pltpu.SemaphoreType.DMA((4,)),
        ],
        compiler_params=pltpu.CompilerParams(vmem_limit_bytes=16 * MIB),
        cost_estimate=pl.CostEstimate(flops=300_000_000, bytes_accessed=8 * MIB, transcendentals=0),
        name="scatter_own",
    )(got, factor, rest_m, rest_g)


def merge_kernel(got, first, first_steps, left3, right2, weight, og, acts_early, out, acts_out,
                 grid, ints, picks, done, weight_in, og_in, acts_in, sem, out_sem, acts_sem):
    late = last_half()
    fetch = [
        pltpu.make_async_copy(weight, weight_in, acts_sem.at[0]),
        pltpu.make_async_copy(og, og_in, acts_sem.at[1]),
    ]

    @pl.when(late)
    def _():
        for c in fetch:
            c.start()

    to_scalars, total = gather_meta(got, ints, picks, sem)
    grid[...] = first[...]
    s = 2.0 * got.shape[0] / (total + first_steps[0, 0])
    to_scalars.wait()
    add_islands(got, grid, picks)
    pairs = grid.shape[1] // 8192
    width = 256 * GROUP
    group = lane_group((8, 128))
    copies = []
    for q in range(pairs // (2 * GROUP)):
        parts = []
        for k in range(2 * GROUP):
            tiles = []
            for r in range(8):
                at = 1024 * (r * pairs + 2 * GROUP * q + k)
                tiles.append(untwist(grid[0, at:at + 1024].reshape(8, 128), group))
            parts.append(jnp.concatenate(tiles, 0))
        hi, lo = split(jnp.concatenate(parts, 1))
        z = dot(left3[...], jnp.concatenate([hi, lo, hi], 0)) * s
        z = jnp.concatenate([z[:, 128 * k:128 * k + 128] for k in range(2 * GROUP)], 0)
        hi, lo = split(z)
        y = dot(jnp.concatenate([hi, lo], 1), right2[...])
        y = (y[:, :128] + y[:, 128:]).astype(BF)
        for k in range(2 * GROUP):
            at = width * q + 128 * k
            done[:, at:at + 128] = y[64 * k:64 * k + 64]
        at = slice(width * q, width * q + width)
        copies.append(pltpu.make_async_copy(done.at[:, at], out.at[:, at], out_sem.at[q]))
        copies[q].start()

    @pl.when(late)
    def _():
        for c in fetch:
            c.wait()
        acts_in[...] = acts_product(weight_in[...], og_in[...])
        back = pltpu.make_async_copy(acts_in, acts_out, acts_sem.at[2])
        back.start()
        back.wait()

    for c in copies:
        c.wait()


def merge_call(got, first, first_steps, weight, og, acts_early):
    rows, cols = weight.shape
    toks = og.shape[0]
    vm = pl.BlockSpec(memory_space=pltpu.VMEM)
    anyw = pl.BlockSpec(memory_space=pl.ANY)
    islands = got.shape[0]
    return pl.pallas_call(
        merge_kernel,
        in_specs=[vm] * 5 + [anyw] * 3,
        out_specs=[anyw, anyw],
        out_shape=[
            jax.ShapeDtypeStruct((rows, cols), BF),
            jax.ShapeDtypeStruct((rows, toks), BF),
        ],
        input_output_aliases={7: 1},
        scratch_shapes=[
            pltpu.VMEM((1, rows * cols), F32),
            pltpu.VMEM((islands // SHARE, 128), jnp.int32),
            pltpu.SMEM((islands // SHARE, 128), jnp.int32),
            pltpu.VMEM((rows, cols), BF),
            pltpu.VMEM((rows, cols), BF),
            pltpu.VMEM((toks, cols), BF),
            pltpu.VMEM((rows, toks), BF),
            pltpu.SemaphoreType.DMA,
            pltpu.SemaphoreType.DMA((cols // (256 * GROUP),)),
            pltpu.SemaphoreType.DMA((3,)),
        ],
        compiler_params=pltpu.CompilerParams(vmem_limit_bytes=32 * MIB),
        cost_estimate=pl.CostEstimate(flops=1_000_000_000, bytes_accessed=2 * MIB, transcendentals=0),
        name="merge_update",
    )(
        got, first, first_steps, INV_LEFT3_MIRROR, INV_RIGHT2,
        *[pltpu.with_memory_space_constraint(x, pltpu.HBM) for x in (weight, og, acts_early)]
    )


def on_device(weight, acts_t, out_grad, momentum, chosen, counts, steps):
    rows, cols = weight.shape
    islands = lax.axis_size("island")
    shards = lax.axis_size("shard")
    half = islands // 2
    same_core = [[2 * i + c for i in range(half)] for c in range(2)]
    other_core = [(i, i ^ 1) for i in range(islands)]
    momentum = momentum[0]

    grad, squares, og_held, weight_held = grad_call(acts_t, out_grad, weight)
    grad, og_held, weight_held = [
        pltpu.with_memory_space_constraint(x, pltpu.VMEM) for x in (grad, og_held, weight_held)
    ]
    squares = squares + lax.ppermute(squares, "shard", [(i, i ^ 1) for i in range(shards)])
    acts_grad = acts_grad_call(weight_held, og_held)
    squares, acts_grad = lax.optimization_barrier((squares, acts_grad))
    squares = squares + lax.ppermute(squares, "shard", [(i, i ^ 3) for i in range(shards)])
    picks = chosen[0] % (rows * cols // 128)
    own_steps = steps.astype(F32)
    meta = jnp.concatenate([picks.astype(F32), own_steps, jnp.zeros((111,), F32)])
    coefs = coef_call(picks, counts[0], momentum, grad)
    squares, coefs, meta = lax.optimization_barrier((squares, coefs, meta))
    pack_m, pack_g, rest_m, rest_g = coefs

    mean = squares / float(rows * cols * shards)
    factor = jnp.minimum(1.0, 1.0 / jnp.sqrt(mean + 1e-06))
    payload = (0.9 * pack_m + factor * pack_g) * own_steps
    sent = jnp.concatenate([payload.reshape(1, PAY), meta[None]], 1)
    sent = jnp.broadcast_to(sent[None], (half, 1, PAY + 128))
    got = lax.all_to_all(sent, "island", 0, 0, tiled=True, axis_index_groups=same_core)
    swapped = lax.ppermute(got, "island", other_core)

    first, first_steps, momentum_next = scatter_call(got, factor, rest_m, rest_g)
    update, acts_grad = merge_call(swapped, first, first_steps, weight, out_grad, acts_grad)
    return (update, momentum_next[None], acts_grad)


def solution(mesh):
    placed = (
        P("shard", None),
        P("shard", "island"),
        P("island", None),
        P("island", "shard", None),
        P("island", "shard"),
        P("island", "shard"),
        P("island"),
    )
    return jax.shard_map(
        on_device,
        mesh=mesh,
        in_specs=placed,
        out_specs=(P("shard", None), P("island", "shard", None), P("shard", "island")),
        check_vma=False,
    )
```

```python
import functools

import jax
import jax.numpy as jnp
import ml_dtypes
import numpy as np
from jax import lax
from jax.experimental import pallas as pl
from jax.experimental.pallas import tpu as pltpu
from jax.sharding import PartitionSpec as P

BF = jnp.bfloat16
F32 = jnp.float32
SLOTS = 16
PAY = SLOTS * 128
MIB = 1 << 20


def dct_matrix():
    freq = np.arange(64, dtype=np.float64)[:, None]
    place = np.arange(64, dtype=np.float64)[None, :]
    waves = np.cos(np.pi * (2.0 * place + 1.0) * freq / 128.0)
    return np.where(freq == 0.0, 0.125, np.sqrt(2.0 / 64.0)) * waves


def halves(a):
    hi = a.astype(ml_dtypes.bfloat16)
    lo = (a - hi.astype(np.float64)).astype(ml_dtypes.bfloat16)
    return hi, lo


COS = dct_matrix()
COS_HI, COS_LO = halves(COS)
INV_HI, INV_LO = halves(COS.T)


def diagonal(a, copies):
    return np.kron(np.eye(copies), a.astype(np.float64)).astype(ml_dtypes.bfloat16)


FWD_LEFT3 = np.concatenate([COS_HI, COS_HI, COS_LO], 1)
FWD_LEFT2 = np.concatenate([COS_HI, COS_LO], 1)
INV_LEFT3 = np.concatenate([INV_HI, INV_HI, INV_LO], 1)
MIRROR = np.array([8 * r + (8 - u) % 8 for r in range(8) for u in range(8)])
INV_LEFT3_MIRROR = np.concatenate([INV_HI[:, MIRROR], INV_HI[:, MIRROR], INV_LO[:, MIRROR]], 1)
FWD_RIGHT3 = np.concatenate([diagonal(COS_HI.T, 2), diagonal(COS_HI.T, 2), diagonal(COS_LO.T, 2)], 0)
INV_RIGHT3 = np.concatenate([diagonal(COS_HI, 2), diagonal(COS_HI, 2), diagonal(COS_LO, 2)], 0)
INV_RIGHT2 = np.block([
    [diagonal(COS_HI, 2), diagonal(COS_LO, 2)],
    [diagonal(COS_HI, 2), np.zeros((128, 128), ml_dtypes.bfloat16)],
])


def split(x):
    hi = x.astype(BF)
    return hi, (x - hi.astype(F32)).astype(BF)


def dot(a, b):
    return jnp.dot(a, b, preferred_element_type=F32)


PARTS = 2


def grad_kernel(acts, og, weight, grad, squares, og_in, weight_in, acts_in, sem):
    cols = og_in.shape[1]
    width = cols // PARTS
    first = pltpu.make_async_copy(acts, acts_in, sem.at[PARTS])
    first.start()
    parts = []
    for i in range(PARTS):
        at = slice(i * width, (i + 1) * width)
        parts.append(pltpu.make_async_copy(og.at[:, at], og_in.at[:, at], sem.at[i]))
        parts[i].start()
    last = pltpu.make_async_copy(weight, weight_in, sem.at[PARTS + 1])
    last.start()
    first.wait()
    a = acts_in[...]
    total = jnp.zeros((8, 512), F32)
    for i in range(PARTS):
        at = slice(i * width, (i + 1) * width)
        parts[i].wait()
        g = dot(a, og_in[:, at])
        grad[:, at] = g
        g = jnp.sum((g * g).reshape(-1, 8, width), axis=0)
        for k in range(0, width, 512):
            total = total + g[:, k:k + 512]
    squares[...] = jnp.full(squares.shape, jnp.sum(total), F32)
    last.wait()


def grad_call(acts, og, weight):
    rows, toks = acts.shape
    cols = og.shape[1]
    vm = pl.BlockSpec(memory_space=pltpu.VMEM)
    anyw = pl.BlockSpec(memory_space=pl.ANY)
    held = [pltpu.with_memory_space_constraint(x, pltpu.HBM) for x in (acts, og, weight)]
    return pl.pallas_call(
        grad_kernel,
        in_specs=[anyw] * 3,
        out_specs=[vm] * 4,
        out_shape=[
            jax.ShapeDtypeStruct((rows, cols), F32),
            jax.ShapeDtypeStruct((1, 128), F32),
            jax.ShapeDtypeStruct((toks, cols), BF),
            jax.ShapeDtypeStruct((rows, cols), BF),
        ],
        scratch_shapes=[
            pltpu.VMEM((rows, toks), BF),
            pltpu.SemaphoreType.DMA((PARTS + 2,)),
        ],
        compiler_params=pltpu.CompilerParams(vmem_limit_bytes=24 * MIB),
        cost_estimate=pl.CostEstimate(flops=2 * rows * toks * cols, bytes_accessed=6 * MIB, transcendentals=0),
        name="weight_grad",
    )(*held)


def last_half():
    return lax.axis_index("island") >= lax.axis_size("island") // 2


def acts_product(weight, og):
    total = lax.dot_general(og, weight, (((1,), (1,)), ((), ())), preferred_element_type=F32)
    return total.T.astype(BF)


def acts_grad_kernel(weight, og, out):
    @pl.when(jnp.logical_not(last_half()))
    def _():
        out[...] = acts_product(weight[...], og[...])


def acts_grad_call(weight, og):
    rows, cols = weight.shape
    toks = og.shape[0]
    vm = pl.BlockSpec(memory_space=pltpu.VMEM)
    return pl.pallas_call(
        acts_grad_kernel,
        in_specs=[vm, vm],
        out_specs=vm,
        out_shape=jax.ShapeDtypeStruct((rows, toks), BF),
        compiler_params=pltpu.CompilerParams(vmem_limit_bytes=16 * MIB),
        cost_estimate=pl.CostEstimate(flops=2 * rows * toks * cols, bytes_accessed=5 * MIB, transcendentals=0),
        name="acts_grad",
    )(weight, og)


def lane_group(shape):
    return lax.broadcasted_iota(jnp.int32, shape, 1) >> 4


def coef_kernel(picks, counts, momentum, grad, left2, left3, right3, back_left3, back_right3,
                pack_m, pack_g, rest_m, rest_g,
                mom_in, grad_in, side_m, side_g, low, wide):
    pairs = [(picks[j] >> 3) & 63 for j in range(SLOTS)]
    lanes = [pl.ds(pl.multiple_of(p * 128, 128), 128) for p in pairs]
    tops = [pl.ds(pl.multiple_of((picks[j] >> 9) * 8, 8), 8) for j in range(SLOTS)]
    offs = [picks[j] & 7 for j in range(SLOTS)]
    here = [slice(128 * j, 128 * j + 128) for j in range(SLOTS)]
    for j in range(SLOTS):
        mom_in[:, here[j]] = momentum[:, lanes[j]]
        grad_in[:, here[j]] = grad[:, lanes[j]]
    wide[...] = jnp.zeros_like(wide)
    m = mom_in[...]
    g_hi, g_lo = split(grad_in[...])
    side_m[...] = dot(left2[...], jnp.concatenate([m, m], 0))
    side_g[...] = dot(left3[...], jnp.concatenate([g_hi, g_lo, g_hi], 0))
    for j in range(SLOTS):
        low[8 * j:8 * j + 8, :] = side_m[tops[j], here[j]]
        low[128 + 8 * j:136 + 8 * j, :] = side_g[tops[j], here[j]]
    hi, lo = split(low[...])
    low[...] = dot(jnp.concatenate([hi, lo, hi], 1), right3[...])
    group = lane_group((8, 128))
    live = counts[0]
    wants = [jnp.where(j < live, offs[j], 8) for j in range(SLOTS)]
    for base, pack in ((0, pack_m), (128, pack_g)):
        for j in range(SLOTS):
            at = slice(base + 8 * j, base + 8 * j + 8)
            kept = jnp.where(group == wants[j], low[at, :], 0.0)
            low[at, :] = kept
            turned = pltpu.roll(kept, 0, 1, stride=16, stride_axis=0)
            pack[j:j + 1, :] = jnp.sum(turned, axis=0, keepdims=True)
    hi, lo = split(low[...])
    low[...] = dot(jnp.concatenate([hi, lo, hi], 1), back_right3[...])
    for j in range(SLOTS):
        wide[tops[j], 128 * j:128 * j + 128] = low[8 * j:8 * j + 8, :]
        wide[tops[j], PAY + 128 * j:PAY + 128 * j + 128] = low[128 + 8 * j:136 + 8 * j, :]
    hi, lo = split(wide[...])
    wide[...] = dot(back_left3[...], jnp.concatenate([hi, lo, hi], 0))
    cols = grad.shape[1]
    for c in range(0, cols, 1024):
        at = slice(c, c + 1024)
        rest_m[:, at] = 0.9 * momentum[:, at].astype(F32)
        rest_g[:, at] = grad[:, at]
    for j in range(SLOTS):
        rest_m[:, lanes[j]] = rest_m[:, lanes[j]] - 0.9 * wide[:, 128 * j:128 * j + 128]
        rest_g[:, lanes[j]] = rest_g[:, lanes[j]] - wide[:, PAY + 128 * j:PAY + 128 * j + 128]


def coef_call(picks, counts, momentum, grad):
    rows, cols = grad.shape
    vm = pl.BlockSpec(memory_space=pltpu.VMEM)
    sm = pl.BlockSpec(memory_space=pltpu.SMEM)
    return pl.pallas_call(
        coef_kernel,
        in_specs=[sm, sm] + [vm] * 7,
        out_specs=[vm] * 4,
        out_shape=[
            jax.ShapeDtypeStruct((16, 128), F32),
            jax.ShapeDtypeStruct((16, 128), F32),
            jax.ShapeDtypeStruct((rows, cols), F32),
            jax.ShapeDtypeStruct((rows, cols), F32),
        ],
        scratch_shapes=[
            pltpu.VMEM((rows, PAY), BF),
            pltpu.VMEM((rows, PAY), F32),
            pltpu.VMEM((rows, PAY), F32),
            pltpu.VMEM((rows, PAY), F32),
            pltpu.VMEM((256, 128), F32),
            pltpu.VMEM((rows, 2 * PAY), F32),
        ],
        compiler_params=pltpu.CompilerParams(vmem_limit_bytes=24 * MIB),
        cost_estimate=pl.CostEstimate(flops=300_000_000, bytes_accessed=8 * MIB, transcendentals=0),
        name="selected_coefs",
    )(picks, counts, momentum, grad, FWD_LEFT2, FWD_LEFT3, FWD_RIGHT3, INV_LEFT3, INV_RIGHT3)


GROUP = 8
SHARE = 4


def gather_meta(got, ints, picks, sem):
    rows = []
    for a in range(got.shape[0] // SHARE):
        turned = [got[SHARE * a + k, :, PAY:] for k in range(SHARE)]
        turned = [turned[0]] + [pltpu.roll(turned[k], 32 * k, 1) for k in range(1, SHARE)]
        rows.append(sum(turned))
    rows = jnp.concatenate(rows, 0)
    ints[...] = rows.astype(jnp.int32)
    to_scalars = pltpu.make_async_copy(ints, picks, sem)
    to_scalars.start()
    lane = lax.broadcasted_iota(jnp.int32, rows.shape, 1)
    return to_scalars, jnp.sum(jnp.where((lane & 31) == SLOTS, rows, 0.0))


def add_islands(got, grid, picks):
    def some(a, carry):
        for k in range(SHARE):
            i = SHARE * a + k
            places = [pl.ds(pl.multiple_of(picks[a, 32 * k + j] * 128, 128), 128) for j in range(SLOTS)]
            sums = [grid[0, places[j]] + got[i, 0, 128 * j:128 * j + 128] for j in range(SLOTS)]
            for j in range(SLOTS):
                grid[0, places[j]] = sums[j]
        return carry

    lax.fori_loop(0, got.shape[0] // SHARE, some, 0, unroll=4)


def untwist(x, group):
    for k in range(3):
        x = jnp.where((group & (1 << k)) != 0, pltpu.roll(x, 8 - (1 << k), 0), x)
    return pltpu.roll(x, 0, 1, stride=16, stride_axis=0)


def scatter_kernel(got, factor, rest_m, rest_g, grid, steps, rest, ints, picks, rest_out, sem, out_sem):
    to_scalars, total = gather_meta(got, ints, picks, sem)
    steps[...] = jnp.full(steps.shape, total, F32)
    grid[...] = jnp.zeros_like(grid)
    f = factor[:, :1]
    cols = rest_out.shape[1]
    width = cols // 4
    copies = []
    for q in range(4):
        at = slice(width * q, width * q + width)
        rest_out[:, at] = (rest_m[:, at] + f * rest_g[:, at]).astype(BF)
        copies.append(pltpu.make_async_copy(rest_out.at[:, at], rest.at[:, at], out_sem.at[q]))
        copies[q].start()
    to_scalars.wait()
    add_islands(got, grid, picks)
    for c in copies:
        c.wait()


def scatter_call(got, factor, rest_m, rest_g):
    rows, cols = rest_m.shape
    vm = pl.BlockSpec(memory_space=pltpu.VMEM)
    islands = got.shape[0]
    return pl.pallas_call(
        scatter_kernel,
        in_specs=[vm] * 4,
        out_specs=[vm, vm, pl.BlockSpec(memory_space=pl.ANY)],
        out_shape=[
            jax.ShapeDtypeStruct((1, rows * cols), F32),
            jax.ShapeDtypeStruct((1, 128), F32),
            jax.ShapeDtypeStruct((rows, cols), BF),
        ],
        scratch_shapes=[
            pltpu.VMEM((islands // SHARE, 128), jnp.int32),
            pltpu.SMEM((islands // SHARE, 128), jnp.int32),
            pltpu.VMEM((rows, cols), BF),
            pltpu.SemaphoreType.DMA,
            pltpu.SemaphoreType.DMA((4,)),
        ],
        compiler_params=pltpu.CompilerParams(vmem_limit_bytes=16 * MIB),
        cost_estimate=pl.CostEstimate(flops=300_000_000, bytes_accessed=8 * MIB, transcendentals=0),
        name="scatter_own",
    )(got, factor, rest_m, rest_g)


def merge_kernel(got, first, first_steps, left3, right2, weight, og, acts_early, out, acts_out,
                 grid, ints, picks, done, weight_in, og_in, acts_in, sem, out_sem, acts_sem):
    late = last_half()
    fetch = [
        pltpu.make_async_copy(weight, weight_in, acts_sem.at[0]),
        pltpu.make_async_copy(og, og_in, acts_sem.at[1]),
    ]

    @pl.when(late)
    def _():
        for c in fetch:
            c.start()

    to_scalars, total = gather_meta(got, ints, picks, sem)
    grid[...] = first[...]
    s = 2.0 * got.shape[0] / (total + first_steps[0, 0])
    to_scalars.wait()
    add_islands(got, grid, picks)
    pairs = grid.shape[1] // 8192
    width = 256 * GROUP
    group = lane_group((8, 128))
    copies = []
    for q in range(pairs // (2 * GROUP)):
        parts = []
        for k in range(2 * GROUP):
            tiles = []
            for r in range(8):
                at = 1024 * (r * pairs + 2 * GROUP * q + k)
                tiles.append(untwist(grid[0, at:at + 1024].reshape(8, 128), group))
            parts.append(jnp.concatenate(tiles, 0))
        hi, lo = split(jnp.concatenate(parts, 1))
        z = dot(left3[...], jnp.concatenate([hi, lo, hi], 0)) * s
        z = jnp.concatenate([z[:, 128 * k:128 * k + 128] for k in range(2 * GROUP)], 0)
        hi, lo = split(z)
        y = dot(jnp.concatenate([hi, lo], 1), right2[...])
        y = (y[:, :128] + y[:, 128:]).astype(BF)
        for k in range(2 * GROUP):
            at = width * q + 128 * k
            done[:, at:at + 128] = y[64 * k:64 * k + 64]
        at = slice(width * q, width * q + width)
        copies.append(pltpu.make_async_copy(done.at[:, at], out.at[:, at], out_sem.at[q]))
        copies[q].start()

    @pl.when(late)
    def _():
        for c in fetch:
            c.wait()
        acts_in[...] = acts_product(weight_in[...], og_in[...])
        back = pltpu.make_async_copy(acts_in, acts_out, acts_sem.at[2])
        back.start()
        back.wait()

    for c in copies:
        c.wait()


def merge_call(got, first, first_steps, weight, og, acts_early):
    rows, cols = weight.shape
    toks = og.shape[0]
    vm = pl.BlockSpec(memory_space=pltpu.VMEM)
    anyw = pl.BlockSpec(memory_space=pl.ANY)
    islands = got.shape[0]
    return pl.pallas_call(
        merge_kernel,
        in_specs=[vm] * 5 + [anyw] * 3,
        out_specs=[anyw, anyw],
        out_shape=[
            jax.ShapeDtypeStruct((rows, cols), BF),
            jax.ShapeDtypeStruct((rows, toks), BF),
        ],
        input_output_aliases={7: 1},
        scratch_shapes=[
            pltpu.VMEM((1, rows * cols), F32),
            pltpu.VMEM((islands // SHARE, 128), jnp.int32),
            pltpu.SMEM((islands // SHARE, 128), jnp.int32),
            pltpu.VMEM((rows, cols), BF),
            pltpu.VMEM((rows, cols), BF),
            pltpu.VMEM((toks, cols), BF),
            pltpu.VMEM((rows, toks), BF),
            pltpu.SemaphoreType.DMA,
            pltpu.SemaphoreType.DMA((cols // (256 * GROUP),)),
            pltpu.SemaphoreType.DMA((3,)),
        ],
        compiler_params=pltpu.CompilerParams(vmem_limit_bytes=32 * MIB),
        cost_estimate=pl.CostEstimate(flops=1_000_000_000, bytes_accessed=2 * MIB, transcendentals=0),
        name="merge_update",
    )(
        got, first, first_steps, INV_LEFT3_MIRROR, INV_RIGHT2,
        *[pltpu.with_memory_space_constraint(x, pltpu.HBM) for x in (weight, og, acts_early)]
    )


def on_device(weight, acts_t, out_grad, momentum, chosen, counts, steps):
    rows, cols = weight.shape
    islands = lax.axis_size("island")
    shards = lax.axis_size("shard")
    half = islands // 2
    same_core = [[2 * i + c for i in reversed(range(half))] for c in range(2)]
    other_core = [(i, i ^ 1) for i in range(islands)]
    momentum = momentum[0]

    grad, squares, og_held, weight_held = grad_call(acts_t, out_grad, weight)
    grad, og_held, weight_held = [
        pltpu.with_memory_space_constraint(x, pltpu.VMEM) for x in (grad, og_held, weight_held)
    ]
    squares = squares + lax.ppermute(squares, "shard", [(i, i ^ 1) for i in range(shards)])
    acts_grad = acts_grad_call(weight_held, og_held)
    squares, acts_grad = lax.optimization_barrier((squares, acts_grad))
    squares = squares + lax.ppermute(squares, "shard", [(i, i ^ 3) for i in range(shards)])
    picks = chosen[0] % (rows * cols // 128)
    own_steps = steps.astype(F32)
    meta = jnp.concatenate([picks.astype(F32), own_steps, jnp.zeros((111,), F32)])
    coefs = coef_call(picks, counts[0], momentum, grad)
    squares, coefs, meta = lax.optimization_barrier((squares, coefs, meta))
    pack_m, pack_g, rest_m, rest_g = coefs

    mean = squares / float(rows * cols * shards)
    factor = jnp.minimum(1.0, 1.0 / jnp.sqrt(mean + 1e-06))
    payload = (0.9 * pack_m + factor * pack_g) * own_steps
    sent = jnp.concatenate([payload.reshape(1, PAY), meta[None]], 1)
    sent = jnp.broadcast_to(sent[None], (half, 1, PAY + 128))
    got = lax.all_to_all(sent, "island", 0, 0, tiled=True, axis_index_groups=same_core)
    swapped = lax.ppermute(got, "island", other_core)

    first, first_steps, momentum_next = scatter_call(got, factor, rest_m, rest_g)
    update, acts_grad = merge_call(swapped, first, first_steps, weight, out_grad, acts_grad)
    return (update, momentum_next[None], acts_grad)


def solution(mesh):
    placed = (
        P("shard", None),
        P("shard", "island"),
        P("island", None),
        P("island", "shard", None),
        P("island", "shard"),
        P("island", "shard"),
        P("island"),
    )
    return jax.shard_map(
        on_device,
        mesh=mesh,
        in_specs=placed,
        out_specs=(P("shard", None), P("island", "shard", None), P("shard", "island")),
        check_vma=False,
    )
```

```python
import functools

import jax
import jax.numpy as jnp
import ml_dtypes
import numpy as np
from jax import lax
from jax.experimental import pallas as pl
from jax.experimental.pallas import tpu as pltpu
from jax.sharding import PartitionSpec as P

BF = jnp.bfloat16
F32 = jnp.float32
SLOTS = 16
PAY = SLOTS * 128
MIB = 1 << 20


def dct_matrix():
    freq = np.arange(64, dtype=np.float64)[:, None]
    place = np.arange(64, dtype=np.float64)[None, :]
    waves = np.cos(np.pi * (2.0 * place + 1.0) * freq / 128.0)
    return np.where(freq == 0.0, 0.125, np.sqrt(2.0 / 64.0)) * waves


def halves(a):
    hi = a.astype(ml_dtypes.bfloat16)
    lo = (a - hi.astype(np.float64)).astype(ml_dtypes.bfloat16)
    return hi, lo


COS = dct_matrix()
COS_HI, COS_LO = halves(COS)
INV_HI, INV_LO = halves(COS.T)


def diagonal(a, copies):
    return np.kron(np.eye(copies), a.astype(np.float64)).astype(ml_dtypes.bfloat16)


FWD_LEFT3 = np.concatenate([COS_HI, COS_HI, COS_LO], 1)
FWD_LEFT2 = np.concatenate([COS_HI, COS_LO], 1)
INV_LEFT3 = np.concatenate([INV_HI, INV_HI, INV_LO], 1)
MIRROR = np.array([8 * r + (8 - u) % 8 for r in range(8) for u in range(8)])
INV_LEFT3_MIRROR = np.concatenate([INV_HI[:, MIRROR], INV_HI[:, MIRROR], INV_LO[:, MIRROR]], 1)
FWD_RIGHT3 = np.concatenate([diagonal(COS_HI.T, 2), diagonal(COS_HI.T, 2), diagonal(COS_LO.T, 2)], 0)
INV_RIGHT3 = np.concatenate([diagonal(COS_HI, 2), diagonal(COS_HI, 2), diagonal(COS_LO, 2)], 0)
INV_RIGHT2 = np.block([
    [diagonal(COS_HI, 2), diagonal(COS_LO, 2)],
    [diagonal(COS_HI, 2), np.zeros((128, 128), ml_dtypes.bfloat16)],
])


def split(x):
    hi = x.astype(BF)
    return hi, (x - hi.astype(F32)).astype(BF)


def dot(a, b):
    return jnp.dot(a, b, preferred_element_type=F32)


PARTS = 2


def grad_kernel(acts, og, weight, grad, squares, og_in, weight_in, acts_in, sem):
    cols = og_in.shape[1]
    width = cols // PARTS
    first = pltpu.make_async_copy(acts, acts_in, sem.at[PARTS])
    first.start()
    parts = []
    for i in range(PARTS):
        at = slice(i * width, (i + 1) * width)
        parts.append(pltpu.make_async_copy(og.at[:, at], og_in.at[:, at], sem.at[i]))
        parts[i].start()
    last = pltpu.make_async_copy(weight, weight_in, sem.at[PARTS + 1])
    last.start()
    first.wait()
    a = acts_in[...]
    total = jnp.zeros((8, 512), F32)
    for i in range(PARTS):
        at = slice(i * width, (i + 1) * width)
        parts[i].wait()
        g = dot(a, og_in[:, at])
        grad[:, at] = g
        g = jnp.sum((g * g).reshape(-1, 8, width), axis=0)
        for k in range(0, width, 512):
            total = total + g[:, k:k + 512]
    squares[...] = jnp.full(squares.shape, jnp.sum(total), F32)
    last.wait()


def grad_call(acts, og, weight):
    rows, toks = acts.shape
    cols = og.shape[1]
    vm = pl.BlockSpec(memory_space=pltpu.VMEM)
    anyw = pl.BlockSpec(memory_space=pl.ANY)
    held = [pltpu.with_memory_space_constraint(x, pltpu.HBM) for x in (acts, og, weight)]
    return pl.pallas_call(
        grad_kernel,
        in_specs=[anyw] * 3,
        out_specs=[vm] * 4,
        out_shape=[
            jax.ShapeDtypeStruct((rows, cols), F32),
            jax.ShapeDtypeStruct((1, 128), F32),
            jax.ShapeDtypeStruct((toks, cols), BF),
            jax.ShapeDtypeStruct((rows, cols), BF),
        ],
        scratch_shapes=[
            pltpu.VMEM((rows, toks), BF),
            pltpu.SemaphoreType.DMA((PARTS + 2,)),
        ],
        compiler_params=pltpu.CompilerParams(vmem_limit_bytes=24 * MIB),
        cost_estimate=pl.CostEstimate(flops=2 * rows * toks * cols, bytes_accessed=6 * MIB, transcendentals=0),
        name="weight_grad",
    )(*held)


def last_half():
    return lax.axis_index("island") >= lax.axis_size("island") // 2


def acts_product(weight, og):
    total = lax.dot_general(og, weight, (((1,), (1,)), ((), ())), preferred_element_type=F32)
    return total.T.astype(BF)


def acts_grad_kernel(weight, og, out):
    @pl.when(jnp.logical_not(last_half()))
    def _():
        out[...] = acts_product(weight[...], og[...])


def acts_grad_call(weight, og):
    rows, cols = weight.shape
    toks = og.shape[0]
    vm = pl.BlockSpec(memory_space=pltpu.VMEM)
    return pl.pallas_call(
        acts_grad_kernel,
        in_specs=[vm, vm],
        out_specs=vm,
        out_shape=jax.ShapeDtypeStruct((rows, toks), BF),
        compiler_params=pltpu.CompilerParams(vmem_limit_bytes=16 * MIB),
        cost_estimate=pl.CostEstimate(flops=2 * rows * toks * cols, bytes_accessed=5 * MIB, transcendentals=0),
        name="acts_grad",
    )(weight, og)


def lane_group(shape):
    return lax.broadcasted_iota(jnp.int32, shape, 1) >> 4


def coef_kernel(picks, counts, momentum, grad, left2, left3, right3, back_left3, back_right3,
                pack_m, pack_g, rest_m, rest_g,
                mom_in, grad_in, side_m, side_g, low, wide):
    pairs = [(picks[j] >> 3) & 63 for j in range(SLOTS)]
    lanes = [pl.ds(pl.multiple_of(p * 128, 128), 128) for p in pairs]
    tops = [pl.ds(pl.multiple_of((picks[j] >> 9) * 8, 8), 8) for j in range(SLOTS)]
    offs = [picks[j] & 7 for j in range(SLOTS)]
    here = [slice(128 * j, 128 * j + 128) for j in range(SLOTS)]
    for j in range(SLOTS):
        mom_in[:, here[j]] = momentum[:, lanes[j]]
        grad_in[:, here[j]] = grad[:, lanes[j]]
    wide[...] = jnp.zeros_like(wide)
    m = mom_in[...]
    g_hi, g_lo = split(grad_in[...])
    side_m[...] = dot(left2[...], jnp.concatenate([m, m], 0))
    side_g[...] = dot(left3[...], jnp.concatenate([g_hi, g_lo, g_hi], 0))
    for j in range(SLOTS):
        low[8 * j:8 * j + 8, :] = side_m[tops[j], here[j]]
        low[128 + 8 * j:136 + 8 * j, :] = side_g[tops[j], here[j]]
    hi, lo = split(low[...])
    low[...] = dot(jnp.concatenate([hi, lo, hi], 1), right3[...])
    group = lane_group((8, 128))
    live = counts[0]
    wants = [jnp.where(j < live, offs[j], 8) for j in range(SLOTS)]
    for base, pack in ((0, pack_m), (128, pack_g)):
        for j in range(SLOTS):
            at = slice(base + 8 * j, base + 8 * j + 8)
            kept = jnp.where(group == wants[j], low[at, :], 0.0)
            low[at, :] = kept
            turned = pltpu.roll(kept, 0, 1, stride=16, stride_axis=0)
            pack[j:j + 1, :] = jnp.sum(turned, axis=0, keepdims=True)
    hi, lo = split(low[...])
    low[...] = dot(jnp.concatenate([hi, lo, hi], 1), back_right3[...])
    for j in range(SLOTS):
        wide[tops[j], 128 * j:128 * j + 128] = low[8 * j:8 * j + 8, :]
        wide[tops[j], PAY + 128 * j:PAY + 128 * j + 128] = low[128 + 8 * j:136 + 8 * j, :]
    hi, lo = split(wide[...])
    wide[...] = dot(back_left3[...], jnp.concatenate([hi, lo, hi], 0))
    cols = grad.shape[1]
    for c in range(0, cols, 1024):
        at = slice(c, c + 1024)
        rest_m[:, at] = 0.9 * momentum[:, at].astype(F32)
        rest_g[:, at] = grad[:, at]
    for j in range(SLOTS):
        rest_m[:, lanes[j]] = rest_m[:, lanes[j]] - 0.9 * wide[:, 128 * j:128 * j + 128]
        rest_g[:, lanes[j]] = rest_g[:, lanes[j]] - wide[:, PAY + 128 * j:PAY + 128 * j + 128]


def coef_call(picks, counts, momentum, grad):
    rows, cols = grad.shape
    vm = pl.BlockSpec(memory_space=pltpu.VMEM)
    sm = pl.BlockSpec(memory_space=pltpu.SMEM)
    return pl.pallas_call(
        coef_kernel,
        in_specs=[sm, sm] + [vm] * 7,
        out_specs=[vm] * 4,
        out_shape=[
            jax.ShapeDtypeStruct((16, 128), F32),
            jax.ShapeDtypeStruct((16, 128), F32),
            jax.ShapeDtypeStruct((rows, cols), F32),
            jax.ShapeDtypeStruct((rows, cols), F32),
        ],
        scratch_shapes=[
            pltpu.VMEM((rows, PAY), BF),
            pltpu.VMEM((rows, PAY), F32),
            pltpu.VMEM((rows, PAY), F32),
            pltpu.VMEM((rows, PAY), F32),
            pltpu.VMEM((256, 128), F32),
            pltpu.VMEM((rows, 2 * PAY), F32),
        ],
        compiler_params=pltpu.CompilerParams(vmem_limit_bytes=24 * MIB),
        cost_estimate=pl.CostEstimate(flops=300_000_000, bytes_accessed=8 * MIB, transcendentals=0),
        name="selected_coefs",
    )(picks, counts, momentum, grad, FWD_LEFT2, FWD_LEFT3, FWD_RIGHT3, INV_LEFT3, INV_RIGHT3)


GROUP = 8
SHARE = 4


def gather_meta(got, ints, picks, sem):
    rows = []
    for a in range(got.shape[0] // SHARE):
        turned = [got[SHARE * a + k, :, PAY:] for k in range(SHARE)]
        turned = [turned[0]] + [pltpu.roll(turned[k], 32 * k, 1) for k in range(1, SHARE)]
        rows.append(sum(turned))
    rows = jnp.concatenate(rows, 0)
    ints[...] = rows.astype(jnp.int32)
    to_scalars = pltpu.make_async_copy(ints, picks, sem)
    to_scalars.start()
    lane = lax.broadcasted_iota(jnp.int32, rows.shape, 1)
    return to_scalars, jnp.sum(jnp.where((lane & 31) == SLOTS, rows, 0.0))


def add_islands(got, grid, picks):
    def some(a, carry):
        for k in range(SHARE):
            i = SHARE * a + k
            places = [pl.ds(pl.multiple_of(picks[a, 32 * k + j] * 128, 128), 128) for j in range(SLOTS)]
            sums = [grid[0, places[j]] + got[i, 0, 128 * j:128 * j + 128] for j in range(SLOTS)]
            for j in range(SLOTS):
                grid[0, places[j]] = sums[j]
        return carry

    lax.fori_loop(0, got.shape[0] // SHARE, some, 0, unroll=4)


def untwist(x, group):
    for k in range(3):
        x = jnp.where((group & (1 << k)) != 0, pltpu.roll(x, 8 - (1 << k), 0), x)
    return pltpu.roll(x, 0, 1, stride=16, stride_axis=0)


def scatter_kernel(got, factor, rest_m, rest_g, grid, steps, rest, ints, picks, rest_out, sem, out_sem):
    to_scalars, total = gather_meta(got, ints, picks, sem)
    steps[...] = jnp.full(steps.shape, total, F32)
    grid[...] = jnp.zeros_like(grid)
    f = factor[:, :1]
    cols = rest_out.shape[1]
    width = cols // 4
    copies = []
    for q in range(4):
        at = slice(width * q, width * q + width)
        rest_out[:, at] = (rest_m[:, at] + f * rest_g[:, at]).astype(BF)
        copies.append(pltpu.make_async_copy(rest_out.at[:, at], rest.at[:, at], out_sem.at[q]))
        copies[q].start()
    to_scalars.wait()
    add_islands(got, grid, picks)
    for c in copies:
        c.wait()


def scatter_call(got, factor, rest_m, rest_g):
    rows, cols = rest_m.shape
    vm = pl.BlockSpec(memory_space=pltpu.VMEM)
    islands = got.shape[0]
    return pl.pallas_call(
        scatter_kernel,
        in_specs=[vm] * 4,
        out_specs=[vm, vm, pl.BlockSpec(memory_space=pl.ANY)],
        out_shape=[
            jax.ShapeDtypeStruct((1, rows * cols), F32),
            jax.ShapeDtypeStruct((1, 128), F32),
            jax.ShapeDtypeStruct((rows, cols), BF),
        ],
        scratch_shapes=[
            pltpu.VMEM((islands // SHARE, 128), jnp.int32),
            pltpu.SMEM((islands // SHARE, 128), jnp.int32),
            pltpu.VMEM((rows, cols), BF),
            pltpu.SemaphoreType.DMA,
            pltpu.SemaphoreType.DMA((4,)),
        ],
        compiler_params=pltpu.CompilerParams(vmem_limit_bytes=16 * MIB),
        cost_estimate=pl.CostEstimate(flops=300_000_000, bytes_accessed=8 * MIB, transcendentals=0),
        name="scatter_own",
    )(got, factor, rest_m, rest_g)


def merge_kernel(got, first, first_steps, left3, right2, weight, og, acts_early, out, acts_out,
                 grid, ints, picks, done, weight_in, og_in, acts_in, sem, out_sem, acts_sem):
    late = last_half()
    fetch = [
        pltpu.make_async_copy(weight, weight_in, acts_sem.at[0]),
        pltpu.make_async_copy(og, og_in, acts_sem.at[1]),
    ]

    @pl.when(late)
    def _():
        for c in fetch:
            c.start()

    to_scalars, total = gather_meta(got, ints, picks, sem)
    grid[...] = first[...]
    s = 2.0 * got.shape[0] / (total + first_steps[0, 0])
    to_scalars.wait()
    add_islands(got, grid, picks)
    pairs = grid.shape[1] // 8192
    width = 256 * GROUP
    group = lane_group((8, 128))
    copies = []
    for q in range(pairs // (2 * GROUP)):
        parts = []
        for k in range(2 * GROUP):
            tiles = []
            for r in range(8):
                at = 1024 * (r * pairs + 2 * GROUP * q + k)
                tiles.append(untwist(grid[0, at:at + 1024].reshape(8, 128), group))
            parts.append(jnp.concatenate(tiles, 0))
        hi, lo = split(jnp.concatenate(parts, 1))
        z = dot(left3[...], jnp.concatenate([hi, lo, hi], 0)) * s
        z = jnp.concatenate([z[:, 128 * k:128 * k + 128] for k in range(2 * GROUP)], 0)
        hi, lo = split(z)
        y = dot(jnp.concatenate([hi, lo], 1), right2[...])
        y = (y[:, :128] + y[:, 128:]).astype(BF)
        for k in range(2 * GROUP):
            at = width * q + 128 * k
            done[:, at:at + 128] = y[64 * k:64 * k + 64]
        at = slice(width * q, width * q + width)
        copies.append(pltpu.make_async_copy(done.at[:, at], out.at[:, at], out_sem.at[q]))
        copies[q].start()

    @pl.when(late)
    def _():
        for c in fetch:
            c.wait()
        acts_in[...] = acts_product(weight_in[...], og_in[...])
        back = pltpu.make_async_copy(acts_in, acts_out, acts_sem.at[2])
        back.start()
        back.wait()

    for c in copies:
        c.wait()


def merge_call(got, first, first_steps, weight, og, acts_early):
    rows, cols = weight.shape
    toks = og.shape[0]
    vm = pl.BlockSpec(memory_space=pltpu.VMEM)
    anyw = pl.BlockSpec(memory_space=pl.ANY)
    islands = got.shape[0]
    return pl.pallas_call(
        merge_kernel,
        in_specs=[vm] * 5 + [anyw] * 3,
        out_specs=[anyw, anyw],
        out_shape=[
            jax.ShapeDtypeStruct((rows, cols), BF),
            jax.ShapeDtypeStruct((rows, toks), BF),
        ],
        input_output_aliases={7: 1},
        scratch_shapes=[
            pltpu.VMEM((1, rows * cols), F32),
            pltpu.VMEM((islands // SHARE, 128), jnp.int32),
            pltpu.SMEM((islands // SHARE, 128), jnp.int32),
            pltpu.VMEM((rows, cols), BF),
            pltpu.VMEM((rows, cols), BF),
            pltpu.VMEM((toks, cols), BF),
            pltpu.VMEM((rows, toks), BF),
            pltpu.SemaphoreType.DMA,
            pltpu.SemaphoreType.DMA((cols // (256 * GROUP),)),
            pltpu.SemaphoreType.DMA((3,)),
        ],
        compiler_params=pltpu.CompilerParams(vmem_limit_bytes=32 * MIB),
        cost_estimate=pl.CostEstimate(flops=1_000_000_000, bytes_accessed=2 * MIB, transcendentals=0),
        name="merge_update",
    )(
        got, first, first_steps, INV_LEFT3_MIRROR, INV_RIGHT2,
        *[pltpu.with_memory_space_constraint(x, pltpu.HBM) for x in (weight, og, acts_early)]
    )


def on_device(weight, acts_t, out_grad, momentum, chosen, counts, steps):
    rows, cols = weight.shape
    islands = lax.axis_size("island")
    shards = lax.axis_size("shard")
    half = islands // 2
    same_core = [[2 * (4 * z + y) + c for z in (4, 5, 6, 7, 0, 1, 2, 3) for y in (3, 2, 1, 0)] for c in range(2)]
    other_core = [(i, i ^ 1) for i in range(islands)]
    momentum = momentum[0]

    grad, squares, og_held, weight_held = grad_call(acts_t, out_grad, weight)
    grad, og_held, weight_held = [
        pltpu.with_memory_space_constraint(x, pltpu.VMEM) for x in (grad, og_held, weight_held)
    ]
    squares = squares + lax.ppermute(squares, "shard", [(i, i ^ 1) for i in range(shards)])
    acts_grad = acts_grad_call(weight_held, og_held)
    squares, acts_grad = lax.optimization_barrier((squares, acts_grad))
    squares = squares + lax.ppermute(squares, "shard", [(i, i ^ 3) for i in range(shards)])
    picks = chosen[0] % (rows * cols // 128)
    own_steps = steps.astype(F32)
    meta = jnp.concatenate([picks.astype(F32), own_steps, jnp.zeros((111,), F32)])
    coefs = coef_call(picks, counts[0], momentum, grad)
    squares, coefs, meta = lax.optimization_barrier((squares, coefs, meta))
    pack_m, pack_g, rest_m, rest_g = coefs

    mean = squares / float(rows * cols * shards)
    factor = jnp.minimum(1.0, 1.0 / jnp.sqrt(mean + 1e-06))
    payload = (0.9 * pack_m + factor * pack_g) * own_steps
    sent = jnp.concatenate([payload.reshape(1, PAY), meta[None]], 1)
    sent = jnp.broadcast_to(sent[None], (half, 1, PAY + 128))
    got = lax.all_to_all(sent, "island", 0, 0, tiled=True, axis_index_groups=same_core)
    swapped = lax.ppermute(got, "island", other_core)

    first, first_steps, momentum_next = scatter_call(got, factor, rest_m, rest_g)
    update, acts_grad = merge_call(swapped, first, first_steps, weight, out_grad, acts_grad)
    return (update, momentum_next[None], acts_grad)


def solution(mesh):
    placed = (
        P("shard", None),
        P("shard", "island"),
        P("island", None),
        P("island", "shard", None),
        P("island", "shard"),
        P("island", "shard"),
        P("island"),
    )
    return jax.shard_map(
        on_device,
        mesh=mesh,
        in_specs=placed,
        out_specs=(P("shard", None), P("island", "shard", None), P("shard", "island")),
        check_vma=False,
    )
```

```python
import functools

import jax
import jax.numpy as jnp
import ml_dtypes
import numpy as np
from jax import lax
from jax.experimental import pallas as pl
from jax.experimental.pallas import tpu as pltpu
from jax.sharding import PartitionSpec as P

BF = jnp.bfloat16
F32 = jnp.float32
SLOTS = 16
PAY = SLOTS * 128
MIB = 1 << 20


def dct_matrix():
    freq = np.arange(64, dtype=np.float64)[:, None]
    place = np.arange(64, dtype=np.float64)[None, :]
    waves = np.cos(np.pi * (2.0 * place + 1.0) * freq / 128.0)
    return np.where(freq == 0.0, 0.125, np.sqrt(2.0 / 64.0)) * waves


def halves(a):
    hi = a.astype(ml_dtypes.bfloat16)
    lo = (a - hi.astype(np.float64)).astype(ml_dtypes.bfloat16)
    return hi, lo


COS = dct_matrix()
COS_HI, COS_LO = halves(COS)
INV_HI, INV_LO = halves(COS.T)


def diagonal(a, copies):
    return np.kron(np.eye(copies), a.astype(np.float64)).astype(ml_dtypes.bfloat16)


FWD_LEFT3 = np.concatenate([COS_HI, COS_HI, COS_LO], 1)
FWD_LEFT2 = np.concatenate([COS_HI, COS_LO], 1)
INV_LEFT3 = np.concatenate([INV_HI, INV_HI, INV_LO], 1)
MIRROR = np.array([8 * r + (8 - u) % 8 for r in range(8) for u in range(8)])
INV_LEFT3_MIRROR = np.concatenate([INV_HI[:, MIRROR], INV_HI[:, MIRROR], INV_LO[:, MIRROR]], 1)
FWD_RIGHT3 = np.concatenate([diagonal(COS_HI.T, 2), diagonal(COS_HI.T, 2), diagonal(COS_LO.T, 2)], 0)
INV_RIGHT3 = np.concatenate([diagonal(COS_HI, 2), diagonal(COS_HI, 2), diagonal(COS_LO, 2)], 0)
INV_RIGHT2 = np.block([
    [diagonal(COS_HI, 2), diagonal(COS_LO, 2)],
    [diagonal(COS_HI, 2), np.zeros((128, 128), ml_dtypes.bfloat16)],
])


def split(x):
    hi = x.astype(BF)
    return hi, (x - hi.astype(F32)).astype(BF)


def dot(a, b):
    return jnp.dot(a, b, preferred_element_type=F32)


PARTS = 2


def grad_kernel(acts, og, weight, grad, squares, og_in, weight_in, acts_in, sem):
    cols = og_in.shape[1]
    width = cols // PARTS
    first = pltpu.make_async_copy(acts, acts_in, sem.at[PARTS])
    first.start()
    parts = []
    for i in range(PARTS):
        at = slice(i * width, (i + 1) * width)
        parts.append(pltpu.make_async_copy(og.at[:, at], og_in.at[:, at], sem.at[i]))
        parts[i].start()
    last = pltpu.make_async_copy(weight, weight_in, sem.at[PARTS + 1])
    last.start()
    first.wait()
    a = acts_in[...]
    total = jnp.zeros((8, 512), F32)
    for i in range(PARTS):
        at = slice(i * width, (i + 1) * width)
        parts[i].wait()
        g = dot(a, og_in[:, at])
        grad[:, at] = g
        g = jnp.sum((g * g).reshape(-1, 8, width), axis=0)
        for k in range(0, width, 512):
            total = total + g[:, k:k + 512]
    squares[...] = jnp.full(squares.shape, jnp.sum(total), F32)
    last.wait()


def grad_call(acts, og, weight):
    rows, toks = acts.shape
    cols = og.shape[1]
    vm = pl.BlockSpec(memory_space=pltpu.VMEM)
    anyw = pl.BlockSpec(memory_space=pl.ANY)
    held = [pltpu.with_memory_space_constraint(x, pltpu.HBM) for x in (acts, og, weight)]
    return pl.pallas_call(
        grad_kernel,
        in_specs=[anyw] * 3,
        out_specs=[vm] * 4,
        out_shape=[
            jax.ShapeDtypeStruct((rows, cols), F32),
            jax.ShapeDtypeStruct((1, 128), F32),
            jax.ShapeDtypeStruct((toks, cols), BF),
            jax.ShapeDtypeStruct((rows, cols), BF),
        ],
        scratch_shapes=[
            pltpu.VMEM((rows, toks), BF),
            pltpu.SemaphoreType.DMA((PARTS + 2,)),
        ],
        compiler_params=pltpu.CompilerParams(vmem_limit_bytes=24 * MIB),
        cost_estimate=pl.CostEstimate(flops=2 * rows * toks * cols, bytes_accessed=6 * MIB, transcendentals=0),
        name="weight_grad",
    )(*held)


def last_half():
    return lax.axis_index("island") >= lax.axis_size("island") // 2


def acts_product(weight, og):
    total = lax.dot_general(og, weight, (((1,), (1,)), ((), ())), preferred_element_type=F32)
    return total.T.astype(BF)


def acts_grad_kernel(weight, og, out):
    @pl.when(jnp.logical_not(last_half()))
    def _():
        out[...] = acts_product(weight[...], og[...])


def acts_grad_call(weight, og):
    rows, cols = weight.shape
    toks = og.shape[0]
    vm = pl.BlockSpec(memory_space=pltpu.VMEM)
    return pl.pallas_call(
        acts_grad_kernel,
        in_specs=[vm, vm],
        out_specs=vm,
        out_shape=jax.ShapeDtypeStruct((rows, toks), BF),
        compiler_params=pltpu.CompilerParams(vmem_limit_bytes=16 * MIB),
        cost_estimate=pl.CostEstimate(flops=2 * rows * toks * cols, bytes_accessed=5 * MIB, transcendentals=0),
        name="acts_grad",
    )(weight, og)


def lane_group(shape):
    return lax.broadcasted_iota(jnp.int32, shape, 1) >> 4


def coef_kernel(picks, counts, momentum, grad, left2, left3, right3, back_left3, back_right3,
                pack_m, pack_g, rest_m, rest_g,
                mom_in, grad_in, side_m, side_g, low, wide):
    pairs = [(picks[j] >> 3) & 63 for j in range(SLOTS)]
    lanes = [pl.ds(pl.multiple_of(p * 128, 128), 128) for p in pairs]
    tops = [pl.ds(pl.multiple_of((picks[j] >> 9) * 8, 8), 8) for j in range(SLOTS)]
    offs = [picks[j] & 7 for j in range(SLOTS)]
    here = [slice(128 * j, 128 * j + 128) for j in range(SLOTS)]
    for j in range(SLOTS):
        mom_in[:, here[j]] = momentum[:, lanes[j]]
        grad_in[:, here[j]] = grad[:, lanes[j]]
    wide[...] = jnp.zeros_like(wide)
    m = mom_in[...]
    g_hi, g_lo = split(grad_in[...])
    side_m[...] = dot(left2[...], jnp.concatenate([m, m], 0))
    side_g[...] = dot(left3[...], jnp.concatenate([g_hi, g_lo, g_hi], 0))
    for j in range(SLOTS):
        low[8 * j:8 * j + 8, :] = side_m[tops[j], here[j]]
        low[128 + 8 * j:136 + 8 * j, :] = side_g[tops[j], here[j]]
    hi, lo = split(low[...])
    low[...] = dot(jnp.concatenate([hi, lo, hi], 1), right3[...])
    group = lane_group((8, 128))
    live = counts[0]
    wants = [jnp.where(j < live, offs[j], 8) for j in range(SLOTS)]
    for base, pack in ((0, pack_m), (128, pack_g)):
        for j in range(SLOTS):
            at = slice(base + 8 * j, base + 8 * j + 8)
            kept = jnp.where(group == wants[j], low[at, :], 0.0)
            low[at, :] = kept
            turned = pltpu.roll(kept, 0, 1, stride=16, stride_axis=0)
            pack[j:j + 1, :] = jnp.sum(turned, axis=0, keepdims=True)
    hi, lo = split(low[...])
    low[...] = dot(jnp.concatenate([hi, lo, hi], 1), back_right3[...])
    for j in range(SLOTS):
        wide[tops[j], 128 * j:128 * j + 128] = low[8 * j:8 * j + 8, :]
        wide[tops[j], PAY + 128 * j:PAY + 128 * j + 128] = low[128 + 8 * j:136 + 8 * j, :]
    hi, lo = split(wide[...])
    wide[...] = dot(back_left3[...], jnp.concatenate([hi, lo, hi], 0))
    cols = grad.shape[1]
    for c in range(0, cols, 1024):
        at = slice(c, c + 1024)
        rest_m[:, at] = 0.9 * momentum[:, at].astype(F32)
        rest_g[:, at] = grad[:, at]
    for j in range(SLOTS):
        rest_m[:, lanes[j]] = rest_m[:, lanes[j]] - 0.9 * wide[:, 128 * j:128 * j + 128]
        rest_g[:, lanes[j]] = rest_g[:, lanes[j]] - wide[:, PAY + 128 * j:PAY + 128 * j + 128]


def coef_call(picks, counts, momentum, grad):
    rows, cols = grad.shape
    vm = pl.BlockSpec(memory_space=pltpu.VMEM)
    sm = pl.BlockSpec(memory_space=pltpu.SMEM)
    return pl.pallas_call(
        coef_kernel,
        in_specs=[sm, sm] + [vm] * 7,
        out_specs=[vm] * 4,
        out_shape=[
            jax.ShapeDtypeStruct((16, 128), F32),
            jax.ShapeDtypeStruct((16, 128), F32),
            jax.ShapeDtypeStruct((rows, cols), F32),
            jax.ShapeDtypeStruct((rows, cols), F32),
        ],
        scratch_shapes=[
            pltpu.VMEM((rows, PAY), BF),
            pltpu.VMEM((rows, PAY), F32),
            pltpu.VMEM((rows, PAY), F32),
            pltpu.VMEM((rows, PAY), F32),
            pltpu.VMEM((256, 128), F32),
            pltpu.VMEM((rows, 2 * PAY), F32),
        ],
        compiler_params=pltpu.CompilerParams(vmem_limit_bytes=24 * MIB),
        cost_estimate=pl.CostEstimate(flops=300_000_000, bytes_accessed=8 * MIB, transcendentals=0),
        name="selected_coefs",
    )(picks, counts, momentum, grad, FWD_LEFT2, FWD_LEFT3, FWD_RIGHT3, INV_LEFT3, INV_RIGHT3)


GROUP = 8
SHARE = 4


def gather_meta(got, ints, picks, sem):
    rows = []
    for a in range(got.shape[0] // SHARE):
        turned = [got[SHARE * a + k, :, PAY:] for k in range(SHARE)]
        turned = [turned[0]] + [pltpu.roll(turned[k], 32 * k, 1) for k in range(1, SHARE)]
        rows.append(sum(turned))
    rows = jnp.concatenate(rows, 0)
    ints[...] = rows.astype(jnp.int32)
    to_scalars = pltpu.make_async_copy(ints, picks, sem)
    to_scalars.start()
    lane = lax.broadcasted_iota(jnp.int32, rows.shape, 1)
    return to_scalars, jnp.sum(jnp.where((lane & 31) == SLOTS, rows, 0.0))


def add_islands(got, grid, picks):
    def some(a, carry):
        for k in range(SHARE):
            i = SHARE * a + k
            places = [pl.ds(pl.multiple_of(picks[a, 32 * k + j] * 128, 128), 128) for j in range(SLOTS)]
            sums = [grid[0, places[j]] + got[i, 0, 128 * j:128 * j + 128] for j in range(SLOTS)]
            for j in range(SLOTS):
                grid[0, places[j]] = sums[j]
        return carry

    lax.fori_loop(0, got.shape[0] // SHARE, some, 0, unroll=4)


def untwist(x, group):
    for k in range(3):
        x = jnp.where((group & (1 << k)) != 0, pltpu.roll(x, 8 - (1 << k), 0), x)
    return pltpu.roll(x, 0, 1, stride=16, stride_axis=0)


def scatter_kernel(got, factor, rest_m, rest_g, grid, steps, rest, ints, picks, rest_out, sem, out_sem):
    to_scalars, total = gather_meta(got, ints, picks, sem)
    steps[...] = jnp.full(steps.shape, total, F32)
    grid[...] = jnp.zeros_like(grid)
    f = factor[:, :1]
    cols = rest_out.shape[1]
    width = cols // 4
    copies = []
    for q in range(4):
        at = slice(width * q, width * q + width)
        rest_out[:, at] = (rest_m[:, at] + f * rest_g[:, at]).astype(BF)
        copies.append(pltpu.make_async_copy(rest_out.at[:, at], rest.at[:, at], out_sem.at[q]))
        copies[q].start()
    to_scalars.wait()
    add_islands(got, grid, picks)
    for c in copies:
        c.wait()


def scatter_call(got, factor, rest_m, rest_g):
    rows, cols = rest_m.shape
    vm = pl.BlockSpec(memory_space=pltpu.VMEM)
    islands = got.shape[0]
    return pl.pallas_call(
        scatter_kernel,
        in_specs=[vm] * 4,
        out_specs=[vm, vm, pl.BlockSpec(memory_space=pl.ANY)],
        out_shape=[
            jax.ShapeDtypeStruct((1, rows * cols), F32),
            jax.ShapeDtypeStruct((1, 128), F32),
            jax.ShapeDtypeStruct((rows, cols), BF),
        ],
        scratch_shapes=[
            pltpu.VMEM((islands // SHARE, 128), jnp.int32),
            pltpu.SMEM((islands // SHARE, 128), jnp.int32),
            pltpu.VMEM((rows, cols), BF),
            pltpu.SemaphoreType.DMA,
            pltpu.SemaphoreType.DMA((4,)),
        ],
        compiler_params=pltpu.CompilerParams(vmem_limit_bytes=16 * MIB),
        cost_estimate=pl.CostEstimate(flops=300_000_000, bytes_accessed=8 * MIB, transcendentals=0),
        name="scatter_own",
    )(got, factor, rest_m, rest_g)


def merge_kernel(got, first, first_steps, left3, right2, weight, og, acts_early, out, acts_out,
                 grid, ints, picks, done, weight_in, og_in, acts_in, sem, out_sem, acts_sem):
    late = last_half()
    fetch = [
        pltpu.make_async_copy(weight, weight_in, acts_sem.at[0]),
        pltpu.make_async_copy(og, og_in, acts_sem.at[1]),
    ]

    @pl.when(late)
    def _():
        for c in fetch:
            c.start()

    to_scalars, total = gather_meta(got, ints, picks, sem)
    grid[...] = first[...]
    s = 2.0 * got.shape[0] / (total + first_steps[0, 0])
    to_scalars.wait()
    add_islands(got, grid, picks)
    pairs = grid.shape[1] // 8192
    width = 256 * GROUP
    group = lane_group((8, 128))
    copies = []
    for q in range(pairs // (2 * GROUP)):
        parts = []
        for k in range(2 * GROUP):
            tiles = []
            for r in range(8):
                at = 1024 * (r * pairs + 2 * GROUP * q + k)
                tiles.append(untwist(grid[0, at:at + 1024].reshape(8, 128), group))
            parts.append(jnp.concatenate(tiles, 0))
        hi, lo = split(jnp.concatenate(parts, 1))
        z = dot(left3[...], jnp.concatenate([hi, lo, hi], 0)) * s
        z = jnp.concatenate([z[:, 128 * k:128 * k + 128] for k in range(2 * GROUP)], 0)
        hi, lo = split(z)
        y = dot(jnp.concatenate([hi, lo], 1), right2[...])
        y = (y[:, :128] + y[:, 128:]).astype(BF)
        for k in range(2 * GROUP):
            at = width * q + 128 * k
            done[:, at:at + 128] = y[64 * k:64 * k + 64]
        at = slice(width * q, width * q + width)
        copies.append(pltpu.make_async_copy(done.at[:, at], out.at[:, at], out_sem.at[q]))
        copies[q].start()

    @pl.when(late)
    def _():
        for c in fetch:
            c.wait()
        acts_in[...] = acts_product(weight_in[...], og_in[...])
        back = pltpu.make_async_copy(acts_in, acts_out, acts_sem.at[2])
        back.start()
        back.wait()

    for c in copies:
        c.wait()


def merge_call(got, first, first_steps, weight, og, acts_early):
    rows, cols = weight.shape
    toks = og.shape[0]
    vm = pl.BlockSpec(memory_space=pltpu.VMEM)
    anyw = pl.BlockSpec(memory_space=pl.ANY)
    islands = got.shape[0]
    return pl.pallas_call(
        merge_kernel,
        in_specs=[vm] * 5 + [anyw] * 3,
        out_specs=[anyw, anyw],
        out_shape=[
            jax.ShapeDtypeStruct((rows, cols), BF),
            jax.ShapeDtypeStruct((rows, toks), BF),
        ],
        input_output_aliases={7: 1},
        scratch_shapes=[
            pltpu.VMEM((1, rows * cols), F32),
            pltpu.VMEM((islands // SHARE, 128), jnp.int32),
            pltpu.SMEM((islands // SHARE, 128), jnp.int32),
            pltpu.VMEM((rows, cols), BF),
            pltpu.VMEM((rows, cols), BF),
            pltpu.VMEM((toks, cols), BF),
            pltpu.VMEM((rows, toks), BF),
            pltpu.SemaphoreType.DMA,
            pltpu.SemaphoreType.DMA((cols // (256 * GROUP),)),
            pltpu.SemaphoreType.DMA((3,)),
        ],
        compiler_params=pltpu.CompilerParams(vmem_limit_bytes=32 * MIB),
        cost_estimate=pl.CostEstimate(flops=1_000_000_000, bytes_accessed=2 * MIB, transcendentals=0),
        name="merge_update",
    )(
        got, first, first_steps, INV_LEFT3_MIRROR, INV_RIGHT2,
        *[pltpu.with_memory_space_constraint(x, pltpu.HBM) for x in (weight, og, acts_early)]
    )


def on_device(weight, acts_t, out_grad, momentum, chosen, counts, steps):
    rows, cols = weight.shape
    islands = lax.axis_size("island")
    shards = lax.axis_size("shard")
    half = islands // 2
    same_core = [[2 * (4 * z + y) + c for z in (4, 5, 6, 7, 0, 1, 2, 3) for y in (3, 2, 1, 0)] for c in range(2)]
    other_core = [(i, i ^ 1) for i in range(islands)]
    momentum = momentum[0]

    grad, squares, og_held, weight_held = grad_call(acts_t, out_grad, weight)
    grad, og_held, weight_held = [
        pltpu.with_memory_space_constraint(x, pltpu.VMEM) for x in (grad, og_held, weight_held)
    ]
    squares = squares + lax.ppermute(squares, "shard", [(i, i ^ 3) for i in range(shards)])
    acts_grad = acts_grad_call(weight_held, og_held)
    squares, acts_grad = lax.optimization_barrier((squares, acts_grad))
    squares = squares + lax.ppermute(squares, "shard", [(i, i ^ 1) for i in range(shards)])
    picks = chosen[0] % (rows * cols // 128)
    own_steps = steps.astype(F32)
    meta = jnp.concatenate([picks.astype(F32), own_steps, jnp.zeros((111,), F32)])
    coefs = coef_call(picks, counts[0], momentum, grad)
    squares, coefs, meta = lax.optimization_barrier((squares, coefs, meta))
    pack_m, pack_g, rest_m, rest_g = coefs

    mean = squares / float(rows * cols * shards)
    factor = jnp.minimum(1.0, 1.0 / jnp.sqrt(mean + 1e-06))
    payload = (0.9 * pack_m + factor * pack_g) * own_steps
    sent = jnp.concatenate([payload.reshape(1, PAY), meta[None]], 1)
    sent = jnp.broadcast_to(sent[None], (half, 1, PAY + 128))
    got = lax.all_to_all(sent, "island", 0, 0, tiled=True, axis_index_groups=same_core)
    swapped = lax.ppermute(got, "island", other_core)

    first, first_steps, momentum_next = scatter_call(got, factor, rest_m, rest_g)
    update, acts_grad = merge_call(swapped, first, first_steps, weight, out_grad, acts_grad)
    return (update, momentum_next[None], acts_grad)


def solution(mesh):
    placed = (
        P("shard", None),
        P("shard", "island"),
        P("island", None),
        P("island", "shard", None),
        P("island", "shard"),
        P("island", "shard"),
        P("island"),
    )
    return jax.shard_map(
        on_device,
        mesh=mesh,
        in_specs=placed,
        out_specs=(P("shard", None), P("island", "shard", None), P("shard", "island")),
        check_vma=False,
    )
```
